256 devices in a mesh: dp: 8 (over y, x_lo), seq: 32 (over x_hi, z, core).
Axes of the slice: x: 4 (x_hi: 2, x_lo: 2; x = x_hi * 2 + x_lo), y: 4, z: 8, core: 2. Of those that a mesh axis runs over, the one named last changes fastest.
Arguments:
- inputs: bfloat16 [8, 16384, 768], P('dp', 'seq'), may hold values from -6 to 6
- cotangent: bfloat16 [8, 16384, 768], P('dp', 'seq'), may hold values from -6 to 6
- gain_first: float32 [768], replicated, may hold values from 0.5 to 1.5
- gain_second: float32 [768], replicated, may hold values from 0.5 to 1.5
- value_w: bfloat16 [192, 768], replicated, may hold values from -0.4375 to 0.4375
- gate_w: bfloat16 [192, 768], replicated, may hold values from -0.4375 to 0.4375
- out_w: bfloat16 [192, 768], replicated, may hold values from -0.4375 to 0.4375
- up_w: bfloat16 [192, 3072], replicated, may hold values from -0.4375 to 0.4375
- down_w: bfloat16 [768, 768], replicated, may hold values from -0.21875 to 0.21875
- first_blocks: bfloat16 [64, 256, 256], P('seq'), may hold values from -0.375 to 0.375
- second_blocks: bfloat16 [256, 64, 64], P('seq'), may hold values from -0.75 to 0.75
Outputs:
- layer_out: bfloat16 [8, 16384, 768], P('dp', 'seq')
- grad_input: bfloat16 [8, 16384, 768], P('dp', 'seq')
- grad_value_w: float32 [192, 768], P(None, ('dp', 'seq'))
- grad_gate_w: float32 [192, 768], P(None, ('dp', 'seq'))
- grad_out_w: float32 [192, 768], P(None, ('dp', 'seq'))
- grad_up_w: float32 [192, 3072], P(None, ('dp', 'seq'))
- grad_down_w: float32 [768, 768], P(None, ('dp', 'seq'))
- grad_gain_first: float32 [768], P(('dp', 'seq'))
- grad_gain_second: float32 [768], P(('dp', 'seq'))
- grad_first_blocks: float32 [64, 256, 256], P('seq')
- grad_second_blocks: float32 [256, 64, 64], P('seq')
The draws below stay inside these ranges and needn't reach their ends.
All inputs are finite; a program needn't handle non-finite values.
Results may differ from the reference program's by a relative error of at most 0.025.
Values may be sent and summed in bfloat16 or wider, within the bound.
A program may use at most 128 MiB of HBM per device.

```python
import math
import jax
import jax.numpy as jnp
from jax import lax

D = 768
NBLK = 4
DB = 192
HB = 768
BLOCK = 256
LOGS = 8
LENGTH = 16384
NA = 64


def spiked(array, key, source, target, shards_of, factor):
    owner, partner = [(jnp.arange(array.shape[position]) // (array.shape[position] // shards_of)).reshape([-1 if axis == position else 1 for axis in range(array.ndim)]) for position in (source, target)]
    chosen = jax.random.permutation(key, shards_of)[partner]
    strong = (owner == chosen) | (owner == (partner + shards_of // 2) % shards_of)
    return jnp.where(strong, factor * array, array)


def level_of(key, extent, cuts, smallest, high):
    def one(dim, parts):
        heights = jax.random.uniform(jax.random.fold_in(jax.random.fold_in(key, 6), dim), (parts,), jnp.float32, smallest / len(cuts), high / len(cuts))
        return jnp.repeat(jnp.exp(heights), extent[dim] // parts).reshape((-1,) + (1,) * (len(extent) - dim - 1))

    loudness = one(*cuts[0])
    for cut in cuts[1:]:
        loudness = loudness * one(*cut)
    return loudness


def centred(own_key, extent, deviation, bound, cuts=(), dtype=jnp.bfloat16):
    loudness = level_of(own_key, extent, cuts, -0.22, 0.18) if cuts else 1.0
    array = jax.random.normal(own_key, extent, jnp.float32) * deviation * loudness
    return jnp.minimum(jnp.maximum(array, -bound), bound).astype(dtype)


def gaussian_with(key, extent, scale, bound, pieces, heavy, dtype=jnp.bfloat16):
    values = scale * jax.random.normal(key, extent, jnp.float32)
    if pieces:
        values = values * level_of(key, extent, pieces, -0.22, 0.18)
    return jnp.clip(spiked(values, jax.random.fold_in(key, 3), *heavy), -bound, bound).astype(dtype)


def setup_inputs(seed: int = 0) -> dict:
    keys = jax.random.split(jax.random.key(seed), 12)
    inputs = centred(keys[0], (LOGS, LENGTH, D), 1.0, 6.0, ((0, 8), (1, 32)))
    cotangent = gaussian_with(keys[1], (LOGS, LENGTH, D), 1.0, 6.0, ((0, 8), (1, 32)), (1, 2, 32, 2.75))
    gain_first = jnp.clip(1.0 + 0.1 * jax.random.normal(keys[2], (D,), jnp.float32), 0.5, 1.5)
    gain_second = jnp.clip(1.0 + 0.1 * jax.random.normal(keys[3], (D,), jnp.float32), 0.5, 1.5)
    value_w = centred(keys[4], (DB, D), DB ** -0.5, 0.4375)
    gate_w = centred(keys[5], (DB, D), DB ** -0.5, 0.4375)
    out_w = centred(keys[6], (DB, D), DB ** -0.5, 0.4375)
    up_w = centred(keys[7], (DB, NBLK * HB), DB ** -0.5, 0.4375)
    down_w = centred(keys[8], (HB, D), HB ** -0.5, 0.21875)
    first_blocks = centred(keys[9], (NA, BLOCK, BLOCK), BLOCK ** -0.5, 0.375, ((0, 32),))
    second_blocks = centred(keys[10], (BLOCK, NA, NA), NA ** -0.5, 0.75, ((0, 32),))
    return dict(inputs=inputs, cotangent=cotangent, gain_first=gain_first, gain_second=gain_second, value_w=value_w, gate_w=gate_w, out_w=out_w, up_w=up_w, down_w=down_w, first_blocks=first_blocks, second_blocks=second_blocks)


EPS = 1e-06

def gelu_exact(values):
    return jax.nn.gelu(values, approximate=False)

def normalize(rows_in, gain_vec):
    factor = lax.rsqrt(lax.optimization_barrier(jnp.mean(rows_in * rows_in, axis=-1, keepdims=True)) + EPS)
    unit_rows = rows_in * factor
    return (unit_rows, factor, (unit_rows * gain_vec).astype(jnp.bfloat16))

def norm_back(grad_in, unit_rows, factor, gain_vec):
    scaled = grad_in * gain_vec
    back_rows = factor * (scaled - unit_rows * lax.optimization_barrier(jnp.mean(scaled * unit_rows, axis=-1, keepdims=True)))
    return (back_rows, lax.optimization_barrier(jnp.sum(grad_in * unit_rows, axis=0)))

def blocked(act_in, weight):
    row_count = act_in.shape[0]
    width_in = weight.shape[0]
    wide_w = weight.astype(jnp.float32).reshape(width_in, NBLK, -1)
    split = act_in.astype(jnp.float32).reshape(row_count, NBLK, width_in)
    return jnp.einsum('rnd,dne->rne', split, wide_w).reshape(row_count, -1)

def blocked_back(grads, weight):
    row_count = grads.shape[0]
    width_in = weight.shape[0]
    wide_w = weight.astype(jnp.float32).reshape(width_in, NBLK, -1)
    split = grads.astype(jnp.float32).reshape(row_count, NBLK, -1)
    return jnp.einsum('rne,dne->rnd', split, wide_w).reshape(row_count, -1)

def blocked_grad(act_in, grads):
    row_count = act_in.shape[0]
    left = act_in.astype(jnp.float32).reshape(row_count, NBLK, -1)
    right = grads.astype(jnp.float32).reshape(row_count, NBLK, -1)
    return jnp.einsum('rnd,rne->dne', left, right).reshape(left.shape[2], -1)

def reference(inputs, cotangent, gain_first, gain_second, value_w, gate_w, out_w, up_w, down_w, first_blocks, second_blocks):
    first_f = first_blocks.astype(jnp.float32)
    second_f = second_blocks.astype(jnp.float32)

    def one_log(log_pair):
        rows_bf, grad_rows = log_pair
        rows_in = rows_bf.astype(jnp.float32)
        unit_first, factor_first, normed_first = normalize(rows_in, gain_first)
        value_rows = blocked(normed_first, value_w).astype(jnp.bfloat16)
        gate_rows = blocked(normed_first, gate_w).astype(jnp.bfloat16)
        value_grid = value_rows.reshape(NA, BLOCK, D)
        first_mix = jnp.einsum('ibk,ikc->ibc', first_f, value_grid.astype(jnp.float32)).astype(jnp.bfloat16)
        mixed_grid = jnp.einsum('bij,jbc->ibc', second_f, first_mix.astype(jnp.float32)).astype(jnp.bfloat16)
        mixed_rows = mixed_grid.reshape(LENGTH, D)
        y_rows = (gate_rows.astype(jnp.float32) * mixed_rows.astype(jnp.float32)).astype(jnp.bfloat16)
        mid_rows = (rows_in + blocked(y_rows, out_w)).astype(jnp.bfloat16)
        mid_f = mid_rows.astype(jnp.float32)
        unit_second, factor_second, normed_second = normalize(mid_f, gain_second)
        hidden_pre = blocked(normed_second, up_w)
        act_f, gelu_back = jax.vjp(gelu_exact, hidden_pre)
        act_rows = act_f.astype(jnp.bfloat16)
        layer_rows = (mid_f + blocked(act_rows, down_w)).astype(jnp.bfloat16)
        d_act = blocked_back(grad_rows, down_w)
        d_pre = gelu_back(d_act)[0].astype(jnp.bfloat16)
        grad_down = blocked_grad(act_rows, grad_rows)
        grad_up = blocked_grad(normed_second, d_pre)
        d_second = blocked_back(d_pre, up_w)
        d_mid_norm, gain_two = norm_back(d_second, unit_second, factor_second, gain_second)
        d_mid = (grad_rows.astype(jnp.float32) + d_mid_norm).astype(jnp.bfloat16)
        grad_out = blocked_grad(y_rows, d_mid)
        d_y = blocked_back(d_mid, out_w)
        d_gate = (d_y * mixed_rows.astype(jnp.float32)).astype(jnp.bfloat16)
        d_mixed = (d_y * gate_rows.astype(jnp.float32)).astype(jnp.bfloat16)
        d_mixed_grid = d_mixed.reshape(NA, BLOCK, D).astype(jnp.float32)
        d_first = jnp.einsum('bij,ibc->jbc', second_f, d_mixed_grid).astype(jnp.bfloat16)
        grad_second = jnp.einsum('ibc,jbc->bij', d_mixed_grid, first_mix.astype(jnp.float32))
        d_first_f = d_first.astype(jnp.float32)
        d_value = jnp.einsum('ibk,ibc->ikc', first_f, d_first_f).astype(jnp.bfloat16).reshape(LENGTH, D)
        grad_first = jnp.einsum('ibc,ikc->ibk', d_first_f, value_grid.astype(jnp.float32))
        grad_value = blocked_grad(normed_first, d_value)
        grad_gate = blocked_grad(normed_first, d_gate)
        d_first_norm = blocked_back(d_value, value_w) + blocked_back(d_gate, gate_w)
        d_in_norm, gain_one = norm_back(d_first_norm, unit_first, factor_first, gain_first)
        grad_rows_in = (d_mid.astype(jnp.float32) + d_in_norm).astype(jnp.bfloat16)
        return (layer_rows, grad_rows_in, grad_value, grad_gate, grad_out, grad_up, grad_down, gain_one, gain_two, grad_first, grad_second)
    result = lax.map(one_log, (inputs, cotangent))
    row_scale = 1.0 / math.sqrt(LOGS * LENGTH)
    mix_scale = 1.0 / math.sqrt(LOGS * D)
    return (result[0], result[1], lax.optimization_barrier(jnp.sum(result[2], axis=0)) * row_scale, lax.optimization_barrier(jnp.sum(result[3], axis=0)) * row_scale, lax.optimization_barrier(jnp.sum(result[4], axis=0)) * row_scale, lax.optimization_barrier(jnp.sum(result[5], axis=0)) * row_scale, lax.optimization_barrier(jnp.sum(result[6], axis=0)) * row_scale, lax.optimization_barrier(jnp.sum(result[7], axis=0)) * row_scale, lax.optimization_barrier(jnp.sum(result[8], axis=0)) * row_scale, lax.optimization_barrier(jnp.sum(result[9], axis=0)) * mix_scale, lax.optimization_barrier(jnp.sum(result[10], axis=0)) * mix_scale)
```

```python
import functools
import math

import jax
import jax.numpy as jnp
import numpy as np
from jax import lax
from jax.experimental import pallas as pl
from jax.experimental.pallas import tpu as pltpu
from jax.sharding import PartitionSpec as P

MESH = pl.DeviceIdType.MESH
F32 = jnp.float32
BF16 = jnp.bfloat16
EPS = 1e-6
NY, NXL, NXH, NZ, NC = 4, 2, 2, 8, 2
NS, ND = NXH * NZ * NC, NY * NXL
D, NB, DB, HB, ROWS, HALF = 768, 4, 192, 768, 512, 256
ROW_SCALE = 1.0 / math.sqrt(131072.0)
MIX_SCALE = 1.0 / math.sqrt(6144.0)
EW, LW = 2048, 256
GL, UL = 1152, 1280
VMEM_LIMIT = 60 * 2**20


def dot(a, b, ca=1, cb=0):
    return lax.dot_general(a, b, (((ca,), (cb,)), ((), ())), preferred_element_type=F32)


def constants():
    one = lambda shape, pairs: _onehot(shape, pairs)
    row, col = [], []
    for ii in range(2):
        for d in range(NS):
            for bl in range(8):
                row.append(ii * 256 + d * 8 + bl)
                col.append(bl * 64 + 2 * d + ii)
    perm_m = one((512, 512), (row, col))
    expand = one((64, 512), (np.arange(512) // 8, np.arange(512)))
    out = np.arange(192)
    c, rem = out // 96, out % 96
    perm3 = one((192, 192), (out, rem // 3 * 6 + c * 3 + rem % 3))
    perm12 = one((192, 192), (out, rem // 12 * 24 + c * 12 + rem % 12))
    dest, t = np.arange(48) // 3, np.arange(48) % 3
    fold = np.concatenate([one((256, 48), (dest * 16 + 3 * f + t, np.arange(48))) for f in range(3)], axis=1)
    z, t = np.arange(96) // 12, np.arange(96) % 12
    low, high = t < 6, t >= 6
    ufold = np.concatenate(
        [
            one((128, 96), ((z * 16 + 9 + t)[low], np.arange(96)[low])),
            one((128, 96), ((z * 16 + 3 + t)[high], np.arange(96)[high])),
        ],
        axis=1,
    )
    return perm_m, expand, perm3, perm12, fold, ufold


def _onehot(shape, pairs):
    array = np.zeros(shape, np.float32)
    array[pairs[0], pairs[1]] = 1.0
    return array


def remote(src, dst, ssem, rsem, device):
    return pltpu.make_async_remote_copy(
        src_ref=src, dst_ref=dst, send_sem=ssem, recv_sem=rsem, device_id=device, device_id_type=MESH
    )


def seq_peer(k, me):
    g, t = k // 8, k % 8
    dx, dc = 1 - g // 2, ((g + 1) // 2) % 2
    dz = 4 + (1 - 2 * (t % 2)) * ((t + 1) // 2)
    xh, z, c = me // 16, (me // 2) % 8, me % 2
    return ((xh + dx) % 2) * 16 + ((z + dz) % 8) * 2 + (c + dc) % 2


def greet(me_s, me_d):
    barrier = pltpu.get_barrier_semaphore()

    def over_seq(k, carry):
        pl.semaphore_signal(barrier, inc=1, device_id={"seq": seq_peer(k, me_s)}, device_id_type=MESH)
        return carry

    def over_dp(k, carry):
        pl.semaphore_signal(barrier, inc=1, device_id={"dp": lax.rem(me_d + k, ND)}, device_id_type=MESH)
        return carry

    lax.fori_loop(0, NS - 1, over_seq, 0)
    lax.fori_loop(1, ND, over_dp, 0)
    pl.semaphore_wait(barrier, NS - 1 + ND - 1)


def a2a_start(sbuf, rbuf, ssem, rsem, me):
    def send(k, carry):
        peer = seq_peer(k, me)
        remote(sbuf.at[peer], rbuf.at[me], ssem, rsem, {"seq": peer}).start()
        return carry

    lax.fori_loop(0, NS - 1, send, 0)
    rbuf[me] = sbuf[me]


def a2a_recv(sbuf, rbuf, ssem, rsem, me):
    part = pl.ds(0, NS - 1)
    remote(sbuf.at[part], rbuf.at[part], ssem, rsem, {"seq": me}).wait_recv()


def a2a_sent(sbuf, rbuf, ssem, rsem, me):
    part = pl.ds(0, NS - 1)
    remote(sbuf.at[part], rbuf.at[part], ssem, rsem, {"seq": me}).wait_send()


def tiles(rows, tile, body):
    def step(t, carry):
        body(pl.ds(pl.multiple_of(t * tile, tile), tile), t)
        return carry

    lax.fori_loop(0, rows // tile, step, 0)


def blk(n, width=DB):
    return slice(n * width, (n + 1) * width)


def unpack_lanes(packed, store):
    count = packed.shape[0]
    for t in range(3):
        v = packed[:, :, 128 * t : 128 * t + 128].astype(F32).reshape(count, 2, 8, 128)
        store(256 * t, v[:, 0].reshape(count * 8, 128))
        store(256 * t + 128, v[:, 1].reshape(count * 8, 128))


def pack_pair(low, high):
    count = low.shape[0] // 8
    both = jnp.concatenate([low.reshape(count, 8, -1), high.reshape(count, 8, -1)], axis=1)
    return both.astype(BF16)


def factor_of(rows):
    return lax.rsqrt(jnp.mean(rows * rows, axis=-1, keepdims=True) + EPS)


def fold_rows(product, acc):
    for r in range(product.shape[0] // 8):
        acc = acc + product[8 * r : 8 * r + 8]
    return acc


def gelu_pair(h):
    size = jnp.abs(h)
    den = 1.0 + (0.3275911 / math.sqrt(2.0)) * size
    t = pl.reciprocal(den, approx=True)
    t = t * (2.0 - den * t)
    e = jnp.exp(-0.5 * (h * h))
    poly = 0.5 * 1.061405429
    for a in (-1.453152027, 1.421413741, -0.284496736, 0.254829592):
        poly = poly * t + 0.5 * a
    q = poly * t * e
    cdf = jnp.where(h >= 0.0, 1.0 - q, q)
    return h * cdf, cdf + h * (e * (1.0 / math.sqrt(2.0 * math.pi)))


def main_kernel(
    x_ref, cot_ref, g1_ref, g2_ref, vw_ref, gw_ref, ow_ref, up_ref, dn_ref, fb_ref, sb_ref,
    pm_ref, ex_ref, p3_ref, p12_ref,
    out_ref, gin_ref, gfirst_ref, gsecond_ref, early_ref, late_ref,
    n1, val, gate, mixed, y, mid, n2, dmid, dgate, df, dval, act, dpre, dact, mm, dmu, t768, hbuf,
    s1, r1, s2, r2, s3, r3, s4, r4, ars, arr, ag, gsec, gain2, tmp,
    ssem, rsem,
):
    me_s, me_d = lax.axis_index("seq"), lax.axis_index("dp")
    greet(me_s, me_d)
    g1, g2 = g1_ref[...], g2_ref[...]

    def norm_first(rows, t):
        v = x_ref[rows, :].astype(F32)
        n1[rows, :] = (v * factor_of(v) * g1).astype(BF16)

    tiles(ROWS, 32, norm_first)
    for n in range(NB):
        val[:, blk(n)] = dot(n1[:, blk(n)], vw_ref[:, blk(n)]).astype(BF16)
    for ct in range(3):
        lanes = slice(256 * ct, 256 * ct + 256)
        pair = [dot(fb_ref[ii], val[ii * HALF : (ii + 1) * HALF, lanes]) for ii in range(2)]
        s1[:, :, lanes] = pack_pair(*pair)
    a2a_start(s1, r1, ssem.at[0], rsem.at[0], me_s)

    for n in range(NB):
        gate[:, blk(n)] = dot(n1[:, blk(n)], gw_ref[:, blk(n)]).astype(BF16)
    spread = dot(pm_ref[...], sb_ref[...]).astype(BF16)
    for ii in range(2):
        wide = dot(spread[ii * HALF : (ii + 1) * HALF], ex_ref[...])
        same = (lax.broadcasted_iota(jnp.int32, wide.shape, 0) & 7) == (
            lax.broadcasted_iota(jnp.int32, wide.shape, 1) & 7
        )
        mm[ii] = jnp.where(same, wide, 0.0).astype(BF16)
    for n in range(NB):
        for ii in range(2):
            dact[ii, n] = dot(cot_ref[ii * HALF : (ii + 1) * HALF, blk(n)], dn_ref[:, blk(n)], 1, 1)

    a2a_recv(s1, r1, ssem.at[0], rsem.at[0], me_s)
    for ii in range(2):
        for ct in range(3):
            lanes = slice(256 * ct, 256 * ct + 256)
            o = dot(mm[ii], r1[:, :, lanes].reshape(NS * 16, 256))
            s2[ii, :, :, 128 * ct : 128 * ct + 128] = pack_pair(o[:, :128], o[:, 128:])
        a2a_start(s2.at[ii], r2.at[ii], ssem.at[1 + ii], rsem.at[1 + ii], me_s)

    gain2[...] = jnp.zeros_like(gain2)

    def token_half(ii, carry):
        base = ii * HALF
        half = pl.ds(pl.multiple_of(base, HALF), HALF)

        def rows_of(rows):
            return pl.ds(pl.multiple_of(base + rows.start, rows.size), rows.size)

        a2a_recv(s2.at[ii], r2.at[ii], ssem.at[1 + ii], rsem.at[1 + ii], me_s)

        def gated(rows, t):
            part = r2[ii, pl.ds(pl.multiple_of(t * 4, 4), 4)]

            def store(lane, v):
                at = (rows_of(rows), slice(lane, lane + 128))
                mixed[at] = v.astype(BF16)
                y[at] = (v * gate[at].astype(F32)).astype(BF16)

            unpack_lanes(part, store)

        tiles(HALF, 32, gated)
        for n in range(NB):
            t768[:, blk(n)] = dot(y[half, blk(n)], ow_ref[:, blk(n)])

        def norm_second(rows, t):
            m = (x_ref[rows_of(rows), :].astype(F32) + t768[rows, :]).astype(BF16)
            mid[rows_of(rows), :] = m
            mf = m.astype(F32)
            n2[rows_of(rows), :] = (mf * factor_of(mf) * g2).astype(BF16)

        tiles(HALF, 32, norm_second)
        for n in range(NB):
            hbuf[...] = dot(n2[half, blk(n)], up_ref[:, blk(n, HB)])

            def gelu(rows, t):
                for lt in range(3):
                    lanes = slice(256 * lt, 256 * lt + 256)
                    wide = slice(n * HB + 256 * lt, n * HB + 256 * lt + 256)
                    value, slope = gelu_pair(hbuf[rows, lanes])
                    act[rows_of(rows), wide] = value.astype(BF16)
                    dpre[rows_of(rows), wide] = (slope * dact[ii, n, rows, lanes]).astype(BF16)

            tiles(HALF, 32, gelu)
            t768[:, blk(n)] = dot(dpre[half, blk(n, HB)], up_ref[:, blk(n, HB)], 1, 1)

        def norm_back_second(rows, t):
            mf = mid[rows_of(rows), :].astype(F32)
            f2 = factor_of(mf)
            u2 = mf * f2
            h2 = t768[rows, :]
            gain2[...] = fold_rows(h2 * u2, gain2[...])
            s = h2 * g2
            d = cot_ref[rows_of(rows), :].astype(F32) + f2 * (s - u2 * jnp.mean(s * u2, axis=-1, keepdims=True))
            dmid[rows_of(rows), :] = d.astype(BF16)

        tiles(HALF, 32, norm_back_second)
        for n in range(NB):
            t768[:, blk(n)] = dot(dmid[half, blk(n)], ow_ref[:, blk(n)], 1, 1)

        def gates_back(rows, t):
            dy = t768[rows, :]
            at = rows_of(rows)
            dgate[at, :] = (dy * mixed[at, :].astype(F32)).astype(BF16)
            dm = dy * gate[at, :].astype(F32)
            for ct in range(3):
                low, high = dm[:, 256 * ct : 256 * ct + 128], dm[:, 256 * ct + 128 : 256 * ct + 256]
                s3[ii, pl.ds(pl.multiple_of(t * 4, 4), 4), :, 128 * ct : 128 * ct + 128] = pack_pair(low, high)

        tiles(HALF, 32, gates_back)
        a2a_start(s3.at[ii], r3.at[ii], ssem.at[3 + ii], rsem.at[3 + ii], me_s)
        return carry

    lax.fori_loop(0, 2, token_half, 0)

    for n in range(NB):
        t = dot(act[:, blk(n, HB)], dn_ref[:, blk(n)])
        out_ref[:, blk(n)] = (mid[:, blk(n)].astype(F32) + t).astype(BF16)
    gain2_t = gain2[...].T
    for n in range(NB):
        tmp[:, 0:D] = dot(cot_ref[:, blk(n)], act[:, blk(n, HB)], 0, 0).astype(BF16)
        tmp[:, D : D + DB] = dot(dgate[:, blk(n)], n1[:, blk(n)], 0, 0).astype(BF16)
        tmp[:, D + DB : GL] = dot(dmid[:, blk(n)], y[:, blk(n)], 0, 0).astype(BF16)
        tmp[:, GL:UL] = jnp.concatenate([gain2_t[blk(n)], jnp.zeros((DB, 120), F32)], axis=1).astype(BF16)
        moved = dot(p3_ref[...], tmp[...]).astype(BF16)
        early_ref[0, n, :, 0:UL] = moved[:96]
        early_ref[1, n, :, 0:UL] = moved[96:]
        grad_up = dot(dpre[:, blk(n, HB)], n2[:, blk(n)], 0, 0).astype(BF16)
        for q in range(4):
            moved = dot(p12_ref[...], grad_up[blk(q)]).astype(BF16)
            early_ref[0, n, :, UL + DB * q : UL + DB * q + DB] = moved[:96]
            early_ref[1, n, :, UL + DB * q : UL + DB * q + DB] = moved[96:]

    for ii in range(2):
        a2a_recv(s3.at[ii], r3.at[ii], ssem.at[3 + ii], rsem.at[3 + ii], me_s)

        def unpack(rows, t):
            def store(lane, v):
                dmu[pl.ds(pl.multiple_of(ii * HALF + t * 32, 32), 32), lane : lane + 128] = v.astype(BF16)

            unpack_lanes(r3[ii, pl.ds(pl.multiple_of(t * 4, 4), 4)], store)

        tiles(HALF, 32, unpack)
    for ct in range(3):
        lanes = slice(256 * ct, 256 * ct + 256)
        o = dot(mm[...].reshape(ROWS, ROWS), dmu[:, lanes], 0, 0)
        s4[:, :, lanes] = o.astype(BF16).reshape(NS, 16, 256)
    a2a_start(s4, r4, ssem.at[5], rsem.at[5], me_s)
    for ii in range(2):
        g = dot(dmu[ii * HALF : (ii + 1) * HALF, :], r1[...].reshape(ROWS, D), 1, 1) * MIX_SCALE
        same = (lax.broadcasted_iota(jnp.int32, g.shape, 0) & 7) == (
            lax.broadcasted_iota(jnp.int32, g.shape, 1) & 7
        )
        g = dot(jnp.where(same, g, 0.0).astype(BF16), ex_ref[...], 1, 1)
        gsec[:, 64 * ii : 64 * ii + 64] = g.astype(BF16)

    a2a_recv(s4, r4, ssem.at[5], rsem.at[5], me_s)
    for ct in range(3):
        lanes = slice(256 * ct, 256 * ct + 256)
        v = r4[:, :, lanes].astype(F32).reshape(NS, 2, 8, 256)
        for ii in range(2):
            df[ii * HALF : (ii + 1) * HALF, lanes] = v[:, ii].reshape(HALF, 256).astype(BF16)
    for ii in range(2):
        half = slice(ii * HALF, (ii + 1) * HALF)
        g = (dot(df[half, :], val[half, :], 1, 1) * MIX_SCALE).astype(BF16)
        for part in range(4):
            ars[4 * ii + part, 0:64, :] = g[64 * part : 64 * part + 64]
    for part in range(ND):
        ars[part, 64:80, 0:128] = gsec[32 * part : 32 * part + 16, :]
        ars[part, 64:80, 128:256] = gsec[32 * part + 16 : 32 * part + 32, :]

    def reduce_send(k, carry):
        peer = lax.rem(me_d + k, ND)
        remote(ars.at[peer], arr.at[me_d], ssem.at[6], rsem.at[6], {"dp": peer}).start()
        return carry

    lax.fori_loop(1, ND, reduce_send, 0)
    arr[me_d] = ars[me_d]

    for ii in range(2):
        half = slice(ii * HALF, (ii + 1) * HALF)
        dval[half, :] = dot(fb_ref[ii], df[half, :], 0, 0).astype(BF16)

    others = pl.ds(0, ND - 1)
    remote(ars.at[others], arr.at[others], ssem.at[6], rsem.at[6], {"dp": me_d}).wait_recv()
    total = arr[0].astype(F32)
    for k in range(1, ND):
        total = total + arr[k].astype(F32)
    ag[me_d] = total.astype(BF16)

    def gather_send(k, carry):
        peer = lax.rem(me_d + k, ND)
        remote(ag.at[me_d], ag.at[me_d], ssem.at[7], rsem.at[7], {"dp": peer}).start()
        return carry

    lax.fori_loop(1, ND, gather_send, 0)

    for n in range(NB):
        for ii in range(2):
            half = slice(ii * HALF, (ii + 1) * HALF)
            dact[ii, 0, :, blk(n)] = dot(dval[half, blk(n)], vw_ref[:, blk(n)], 1, 1) + dot(
                dgate[half, blk(n)], gw_ref[:, blk(n)], 1, 1
            )
    gain2[...] = jnp.zeros_like(gain2)
    for ii in range(2):

        def norm_back_first(rows, t):
            at = pl.ds(pl.multiple_of(ii * HALF + t * 32, 32), 32)
            v = x_ref[at, :].astype(F32)
            f1 = factor_of(v)
            u1 = v * f1
            h1 = dact[ii, 0, rows, :]
            gain2[...] = fold_rows(h1 * u1, gain2[...])
            s = h1 * g1
            d = dmid[at, :].astype(F32) + f1 * (s - u1 * jnp.mean(s * u1, axis=-1, keepdims=True))
            gin_ref[at, :] = d.astype(BF16)

        tiles(HALF, 32, norm_back_first)
    gain1_t = gain2[...].T
    for n in range(NB):
        grad_v = dot(dval[:, blk(n)], n1[:, blk(n)], 0, 0)
        piece = jnp.concatenate([grad_v, gain1_t[blk(n)], jnp.zeros((DB, 56), F32)], axis=1).astype(BF16)
        moved = dot(p3_ref[...], piece).astype(BF16)
        late_ref[0, n] = moved[:96]
        late_ref[1, n] = moved[96:]

    remote(ag.at[others], ag.at[others], ssem.at[7], rsem.at[7], {"dp": me_d}).wait_recv()
    for part in range(ND):
        ii, at = part // 4, 64 * (part % 4)
        gfirst_ref[ii, at : at + 64, :] = ag[part, 0:64, :].astype(F32)
        dmu[32 * part : 32 * part + 16, 0:128] = ag[part, 64:80, 0:128]
        dmu[32 * part + 16 : 32 * part + 32, 0:128] = ag[part, 64:80, 128:256]
    gsecond_ref[...] = dot(pm_ref[0:HALF, :], dmu[0:HALF, 0:64], 0, 0) + dot(
        pm_ref[HALF:ROWS, :], dmu[0:HALF, 64:128], 0, 0
    )

    a2a_sent(s1, r1, ssem.at[0], rsem.at[0], me_s)
    for ii in range(2):
        a2a_sent(s2.at[ii], r2.at[ii], ssem.at[1 + ii], rsem.at[1 + ii], me_s)
        a2a_sent(s3.at[ii], r3.at[ii], ssem.at[3 + ii], rsem.at[3 + ii], me_s)
    a2a_sent(s4, r4, ssem.at[5], rsem.at[5], me_s)
    remote(ars.at[others], arr.at[others], ssem.at[6], rsem.at[6], {"dp": me_d}).wait_send()
    remote(ag.at[others], ag.at[others], ssem.at[7], rsem.at[7], {"dp": me_d}).wait_send()


def reduce_kernel(
    early_ref, late_ref, fold_ref, ufold_ref,
    gv_ref, gg_ref, go_ref, gu_ref, gd_ref, g1_ref, g2_ref,
    core_e, core_l, ys_e, ys_l, yr_e, yr_l, xs_d, xs_u, xs_l, xr_d, xr_u, xr_l, fs, fr, fsl, frl, full, full_l,
    ssem, rsem,
):
    me_s, me_d = lax.axis_index("seq"), lax.axis_index("dp")
    greet(me_s, me_d)
    yy, xl = me_d // NXL, lax.rem(me_d, NXL)
    hz, core = me_s // NC, lax.rem(me_s, NC)
    mate = {"seq": hz * NC + 1 - core}

    first = [
        remote(early_ref.at[1 - core], core_e, ssem.at[0], rsem.at[0], mate),
        remote(late_ref.at[1 - core], core_l, ssem.at[1], rsem.at[1], mate),
    ]
    for copy in first:
        copy.start()
    for copy in first:
        copy.wait_recv()
    for n in range(NY):
        ys_e[n] = (early_ref[core, n].astype(F32) + core_e[n].astype(F32)).astype(BF16)
        ys_l[n] = (late_ref[core, n].astype(F32) + core_l[n].astype(F32)).astype(BF16)

    def y_send(k, carry):
        to = lax.rem(yy + k, NY)
        peer = {"dp": to * NXL + xl}
        remote(ys_e.at[to], yr_e.at[yy], ssem.at[2], rsem.at[2], peer).start()
        remote(ys_l.at[to], yr_l.at[yy], ssem.at[3], rsem.at[3], peer).start()
        return carry

    lax.fori_loop(1, NY, y_send, 0)
    yr_e[yy] = ys_e[yy]
    yr_l[yy] = ys_l[yy]
    part = pl.ds(0, NY - 1)
    y_all = [
        remote(ys_e.at[part], yr_e.at[part], ssem.at[2], rsem.at[2], mate),
        remote(ys_l.at[part], yr_l.at[part], ssem.at[3], rsem.at[3], mate),
    ]
    for copy in y_all:
        copy.wait_recv()
    total = yr_e[0].astype(F32)
    total_l = yr_l[0].astype(F32)
    for k in range(1, NY):
        total = total + yr_e[k].astype(F32)
        total_l = total_l + yr_l[k].astype(F32)
    full[...] = total
    full_l[...] = total_l

    for h in range(NXL):
        xs_d[h] = full[48 * h : 48 * h + 48, 0:UL].astype(BF16)
        xs_u[h] = full[:, UL + 384 * h : UL + 384 * h + 384].astype(BF16)
        xs_l[h] = full_l[48 * h : 48 * h + 48, :].astype(BF16)
    beside = {"dp": yy * NXL + 1 - xl}
    second = [
        remote(xs_d.at[1 - xl], xr_d, ssem.at[4], rsem.at[4], beside),
        remote(xs_u.at[1 - xl], xr_u, ssem.at[5], rsem.at[5], beside),
        remote(xs_l.at[1 - xl], xr_l, ssem.at[6], rsem.at[6], beside),
    ]
    for copy in second:
        copy.start()
    for copy in second:
        copy.wait_recv()
    dd = (xs_d[xl].astype(F32) + xr_d[...].astype(F32)).astype(BF16)
    uu = (xs_u[xl].astype(F32) + xr_u[...].astype(F32)).astype(BF16)
    ll = (xs_l[xl].astype(F32) + xr_l[...].astype(F32)).astype(BF16)

    folded = dot(fold_ref[:, 0:48], dd[:, 0:512]) + dot(fold_ref[:, 48:96], dd[:, 512:1024])
    fs[:, :, :] = folded.astype(BF16).reshape(16, 16, 512)
    tail = dot(fold_ref[:, 96:144], dd[:, 1024:1280]).astype(BF16).reshape(16, 16, 256)
    fs[:, :, 0:256] = fs[:, :, 0:256] + tail
    for h in range(NXH):
        u = uu[:, DB * h : DB * h + DB]
        low = dot(ufold_ref[:, 0:96], u).astype(BF16).reshape(8, 16, DB)
        high = dot(ufold_ref[:, 96:192], u).astype(BF16).reshape(8, 16, DB)
        at = slice(8 * h, 8 * h + 8)
        fs[at, :, 0:DB] = fs[at, :, 0:DB] + low
        fs[at, :, 256 : 256 + DB] = fs[at, :, 256 : 256 + DB] + high
    fsl[...] = dot(fold_ref[:, 0:48], ll).astype(BF16).reshape(16, 16, LW)

    def last_send(k, carry):
        to = lax.rem(hz + k, NXH * NZ)
        peer = {"seq": to * NC + core}
        remote(fs.at[to], fr.at[hz], ssem.at[7], rsem.at[7], peer).start()
        remote(fsl.at[to], frl.at[hz], ssem.at[8], rsem.at[8], peer).start()
        return carry

    lax.fori_loop(1, NXH * NZ, last_send, 0)
    fr[hz] = fs[hz]
    frl[hz] = fsl[hz]
    part = pl.ds(0, NXH * NZ - 1)
    last = [
        remote(fs.at[part], fr.at[part], ssem.at[7], rsem.at[7], mate),
        remote(fsl.at[part], frl.at[part], ssem.at[8], rsem.at[8], mate),
    ]
    for copy in last:
        copy.wait_recv()
    total = fr[0].astype(F32)
    total_l = frl[0].astype(F32)
    for k in range(1, NXH * NZ):
        total = total + fr[k].astype(F32)
        total_l = total_l + frl[k].astype(F32)
    across = (total * ROW_SCALE).T
    across_l = (total_l * ROW_SCALE).T
    gd_ref[0:512, :] = across[0:512, 0:3]
    gd_ref[512:768, :] = across[0:256, 3:6]
    gg_ref[...] = across[256:448, 3:6]
    go_ref[0:64, :] = across[448:512, 3:6]
    go_ref[64:192, :] = across[0:128, 6:9]
    gu_ref[:, 0:6] = across[0:192, 9:15]
    gu_ref[:, 6:12] = across[256:448, 9:15]
    g2_ref[...] = jnp.sum(across[128:136, 6:9], axis=0, keepdims=True)
    gv_ref[...] = across_l[0:192, 0:3]
    g1_ref[...] = jnp.sum(across_l[192:200, 0:3], axis=0, keepdims=True)

    for copy in first + y_all + second + last:
        copy.wait_send()


def vmem_specs(count):
    return [pl.BlockSpec(memory_space=pltpu.VMEM)] * count


def body(inputs, cotangent, gain_first, gain_second, value_w, gate_w, out_w, up_w, down_w, first_blocks, second_blocks):
    perm_m, expand, perm3, perm12, fold, ufold = [jnp.asarray(a, BF16) for a in constants()]
    shape = jax.ShapeDtypeStruct
    vm = lambda *s: pltpu.VMEM(s, BF16)
    vf = lambda *s: pltpu.VMEM(s, F32)
    big = lambda: vm(ROWS, D)
    out, gin, gfirst, gsecond, early, late = pl.pallas_call(
        main_kernel,
        out_shape=[
            shape((ROWS, D), BF16), shape((ROWS, D), BF16), shape((2, 256, 256), F32), shape((512, 64), F32),
            shape((2, NB, 96, EW), BF16), shape((2, NB, 96, LW), BF16),
        ],
        in_specs=vmem_specs(15),
        out_specs=vmem_specs(6),
        scratch_shapes=[
            big(), big(), big(), big(), big(), big(), big(), big(), big(), big(), big(),
            vm(ROWS, NB * HB), vm(ROWS, NB * HB), vf(2, NB, HALF, HB),
            vm(2, HALF, ROWS), big(), vf(HALF, D), vf(HALF, HB),
            vm(NS, 16, D), vm(NS, 16, D), vm(2, NS, 16, 384), vm(2, NS, 16, 384),
            vm(2, NS, 16, 384), vm(2, NS, 16, 384), vm(NS, 16, D), vm(NS, 16, D),
            vm(ND, 80, 256), vm(ND, 80, 256), vm(ND, 80, 256), vm(HALF, 128),
            vf(8, D), vm(DB, UL),
            pltpu.SemaphoreType.DMA((8,)), pltpu.SemaphoreType.DMA((8,)),
        ],
        compiler_params=pltpu.CompilerParams(
            collective_id=0, has_side_effects=True, vmem_limit_bytes=VMEM_LIMIT
        ),
    )(
        inputs.reshape(ROWS, D), cotangent.reshape(ROWS, D), gain_first.reshape(1, D), gain_second.reshape(1, D),
        value_w, gate_w, out_w, up_w, down_w, first_blocks, second_blocks.reshape(512, 64),
        perm_m, expand, perm3, perm12,
    )
    gv, gg, go, gu, gd, g1, g2 = pl.pallas_call(
        reduce_kernel,
        out_shape=[
            shape((DB, 3), F32), shape((DB, 3), F32), shape((DB, 3), F32), shape((DB, 12), F32), shape((HB, 3), F32),
            shape((1, 3), F32), shape((1, 3), F32),
        ],
        in_specs=vmem_specs(4),
        out_specs=vmem_specs(7),
        scratch_shapes=[
            vm(NY, 96, EW), vm(NY, 96, LW), vm(NY, 96, EW), vm(NY, 96, LW), vm(NY, 96, EW), vm(NY, 96, LW),
            vm(2, 48, UL), vm(2, 96, 384), vm(2, 48, LW), vm(48, UL), vm(96, 384), vm(48, LW),
            vm(16, 16, 512), vm(16, 16, 512), vm(16, 16, LW), vm(16, 16, LW), vf(96, EW), vf(96, LW),
            pltpu.SemaphoreType.DMA((9,)), pltpu.SemaphoreType.DMA((9,)),
        ],
        compiler_params=pltpu.CompilerParams(
            collective_id=1, has_side_effects=True, vmem_limit_bytes=VMEM_LIMIT
        ),
    )(early, late, fold, ufold)
    return (
        out.reshape(1, ROWS, D), gin.reshape(1, ROWS, D), gv, gg, go, gu, gd, g1.reshape(3), g2.reshape(3),
        gfirst, gsecond.reshape(8, 64, 64),
    )


def solution(mesh):
    tokens, whole = P("dp", "seq", None), P("seq", None, None)
    columns = P(None, ("dp", "seq"))
    gains = P(("dp", "seq"))
    return jax.shard_map(
        body,
        mesh=mesh,
        in_specs=(tokens, tokens, P(), P(), P(), P(), P(), P(), P(), whole, whole),
        out_specs=(tokens, tokens, columns, columns, columns, columns, columns, gains, gains, whole, whole),
        check_vma=False,
    )
```

```python
import functools
import math

import jax
import jax.numpy as jnp
import numpy as np
from jax import lax
from jax.experimental import pallas as pl
from jax.experimental.pallas import tpu as pltpu
from jax.sharding import PartitionSpec as P

MESH = pl.DeviceIdType.MESH
F32 = jnp.float32
BF16 = jnp.bfloat16
EPS = 1e-6
NY, NXL, NXH, NZ, NC = 4, 2, 2, 8, 2
NS, ND = NXH * NZ * NC, NY * NXL
D, NB, DB, HB, ROWS, HALF = 768, 4, 192, 768, 512, 256
ROW_SCALE = 1.0 / math.sqrt(131072.0)
MIX_SCALE = 1.0 / math.sqrt(6144.0)
DL, UL, LW = 1280, 768, 256
GL = 1152
A1, A2, A2B, A3, A3B, A4, GS, GF, CORE, YY, XX, LAST = 0, 3, 6, 7, 8, 11, 14, 16, 18, 21, 24, 27
SEMS = 29
VMEM_LIMIT = 60 * 2**20


def dot(a, b, ca=1, cb=0):
    return lax.dot_general(a, b, (((ca,), (cb,)), ((), ())), preferred_element_type=F32)


def constants():
    one = lambda shape, pairs: _onehot(shape, pairs)
    row, col = [], []
    for ii in range(2):
        for d in range(NS):
            for bl in range(8):
                row.append(ii * 256 + d * 8 + bl)
                col.append(bl * 64 + 2 * d + ii)
    perm_m = one((512, 512), (row, col))
    expand = one((64, 512), (np.arange(512) // 8, np.arange(512)))
    out = np.arange(192)
    c, rem = out // 96, out % 96
    perm3 = one((192, 192), (out, rem // 3 * 6 + c * 3 + rem % 3))
    perm12 = one((192, 192), (out, rem // 12 * 24 + c * 12 + rem % 12))
    dest, t = np.arange(48) // 3, np.arange(48) % 3
    fold = np.concatenate([one((256, 48), (dest * 16 + 3 * f + t, np.arange(48))) for f in range(3)], axis=1)
    z, t = np.arange(96) // 12, np.arange(96) % 12
    low, high = t < 6, t >= 6
    ufold = np.concatenate(
        [
            one((128, 96), ((z * 16 + 9 + t)[low], np.arange(96)[low])),
            one((128, 96), ((z * 16 + 3 + t)[high], np.arange(96)[high])),
        ],
        axis=1,
    )
    return perm_m, expand, perm3, perm12, fold, ufold


def _onehot(shape, pairs):
    array = np.zeros(shape, np.float32)
    array[pairs[0], pairs[1]] = 1.0
    return array


def remote(src, dst, ssem, rsem, device):
    return pltpu.make_async_remote_copy(
        src_ref=src, dst_ref=dst, send_sem=ssem, recv_sem=rsem, device_id=device, device_id_type=MESH
    )


def seq_peer(k, me):
    g, t = k // 8, k % 8
    dx, dc = 1 - g // 2, ((g + 1) // 2) % 2
    dz = 4 + (1 - 2 * (t % 2)) * ((t + 1) // 2)
    xh, z, c = me // 16, (me // 2) % 8, me % 2
    return ((xh + dx) % 2) * 16 + ((z + dz) % 8) * 2 + (c + dc) % 2


def greet(me_s, me_d):
    barrier = pltpu.get_barrier_semaphore()

    def over_seq(k, carry):
        pl.semaphore_signal(barrier, inc=1, device_id={"seq": seq_peer(k, me_s)}, device_id_type=MESH)
        return carry

    def over_dp(k, carry):
        pl.semaphore_signal(barrier, inc=1, device_id={"dp": lax.rem(me_d + k, ND)}, device_id_type=MESH)
        return carry

    lax.fori_loop(0, NS - 1, over_seq, 0)
    lax.fori_loop(1, ND, over_dp, 0)
    return lambda: pl.semaphore_wait(barrier, NS - 1 + ND - 1)


class Exchange:
    def __init__(self, sbuf, rbuf, ssem, rsem, me, lanes=None):
        self.me, self.sems = me, (ssem, rsem)
        self.sbuf, self.rbuf, self.lanes = sbuf, rbuf, lanes

    def at(self, ref, index):
        return ref.at[index] if self.lanes is None else ref.at[index, :, self.lanes]

    def start(self):
        def send(k, carry):
            peer = seq_peer(k, self.me)
            remote(self.at(self.sbuf, peer), self.at(self.rbuf, self.me), *self.sems, {"seq": peer}).start()
            return carry

        lax.fori_loop(0, NS - 1, send, 0)
        if self.lanes is None:
            self.rbuf[self.me] = self.sbuf[self.me]
        else:
            self.rbuf[self.me, :, self.lanes] = self.sbuf[self.me, :, self.lanes]

    def whole(self):
        part = pl.ds(0, NS - 1)
        return remote(self.at(self.sbuf, part), self.at(self.rbuf, part), *self.sems, {"seq": self.me})

    def recv(self):
        self.whole().wait_recv()

    def sent(self):
        self.whole().wait_send()


class Ring:
    def __init__(self, sbuf, rbuf, ssem, rsem, me, count, device, same=False):
        self.sbuf, self.rbuf, self.sems = sbuf, rbuf, (ssem, rsem)
        self.me, self.count, self.device, self.same = me, count, device, same

    def start(self):
        def send(k, carry):
            to = lax.rem(self.me + k, self.count)
            source = self.sbuf.at[self.me if self.same else to]
            remote(source, self.rbuf.at[self.me], *self.sems, self.device(to)).start()
            return carry

        lax.fori_loop(1, self.count, send, 0)
        if not self.same:
            self.rbuf[self.me] = self.sbuf[self.me]

    def whole(self):
        part = pl.ds(0, self.count - 1)
        return remote(self.sbuf.at[part], self.rbuf.at[part], *self.sems, self.device(self.me))

    def recv(self):
        self.whole().wait_recv()

    def sent(self):
        self.whole().wait_send()

    def total(self):
        out = self.rbuf[0].astype(F32)
        for k in range(1, self.count):
            out = out + self.rbuf[k].astype(F32)
        return out


def tiles(rows, tile, body):
    def step(t, carry):
        body(pl.ds(pl.multiple_of(t * tile, tile), tile), t)
        return carry

    lax.fori_loop(0, rows // tile, step, 0)


def blk(n, width=DB):
    return slice(n * width, (n + 1) * width)


def unpack_lanes(packed, store):
    count = packed.shape[0]
    for t in range(3):
        v = packed[:, :, 128 * t : 128 * t + 128].astype(F32).reshape(count, 2, 8, 128)
        store(256 * t, v[:, 0].reshape(count * 8, 128))
        store(256 * t + 128, v[:, 1].reshape(count * 8, 128))


def pack_pair(low, high):
    count = low.shape[0] // 8
    both = jnp.concatenate([low.reshape(count, 8, -1), high.reshape(count, 8, -1)], axis=1)
    return both.astype(BF16)


def factor_of(rows):
    return lax.rsqrt(jnp.mean(rows * rows, axis=-1, keepdims=True) + EPS)


def fold_rows(product, acc):
    for r in range(product.shape[0] // 8):
        acc = acc + product[8 * r : 8 * r + 8]
    return acc


def gelu_pair(h):
    size = jnp.abs(h)
    den = 1.0 + (0.3275911 / math.sqrt(2.0)) * size
    t = pl.reciprocal(den, approx=True)
    t = t * (2.0 - den * t)
    e = jnp.exp(-0.5 * (h * h))
    poly = 0.5 * 1.061405429
    for a in (-1.453152027, 1.421413741, -0.284496736, 0.254829592):
        poly = poly * t + 0.5 * a
    q = poly * t * e
    cdf = jnp.where(h >= 0.0, 1.0 - q, q)
    return h * cdf, cdf + h * (e * (1.0 / math.sqrt(2.0 * math.pi)))


def same_block(shape):
    return (lax.broadcasted_iota(jnp.int32, shape, 0) & 7) == (lax.broadcasted_iota(jnp.int32, shape, 1) & 7)


def main_kernel(
    x_hbm, cot_hbm, g1_ref, g2_ref, vw_hbm, gw_hbm, ow_hbm, up_hbm, dn_hbm, fb_hbm, sb_hbm,
    pm_hbm, ex_hbm, p3_hbm, p12_hbm, fold_hbm, ufold_hbm,
    out_hbm, gin_hbm, mix_ref, early_ref, late_ref,
    x_ref, cot_ref, vw_ref, gw_ref, ow_ref, up_ref, dn_ref, fb_ref, sb_ref,
    pm_ref, ex_ref, p3_ref, p12_ref, fold_ref, ufold_ref, out_ref, gin_ref,
    n1, val, gate, mixed, y, mid, n2, dmid, dgate, df, dval, act, dpre, dact, mm, dmu, t768, hbuf, h1g, gfull,
    s1, r1, s2, r2, s3, r3, s4, r4, gss, gsr, gsa, gfs, gfr, gfa, gsec, gain2, gcol, tmp,
    cs_d, cs_u, cs_l, cr_d, cr_u, cr_l, ys_d, ys_u, ys_l, yr_d, yr_u, yr_l,
    xs_d, xs_u, xs_l, xr_d, xr_u, xr_l, fs, fr, fsl, frl,
    ssem, rsem, lsem,
):
    me_s, me_d = lax.axis_index("seq"), lax.axis_index("dp")
    yy, xl = me_d // NXL, lax.rem(me_d, NXL)
    hz, core = me_s // NC, lax.rem(me_s, NC)
    all_here = greet(me_s, me_d)

    def exchange(sbuf, rbuf, index, lanes=None):
        return Exchange(sbuf, rbuf, ssem.at[index], rsem.at[index], me_s, lanes)

    def lanes_of(ct, width=256):
        return slice(width * ct, width * ct + width)

    ex1 = [exchange(s1, r1, A1 + ct, lanes_of(ct)) for ct in range(3)]
    ex2 = [
        [exchange(s2.at[0], r2.at[0], A2 + ct, lanes_of(ct, 128)) for ct in range(3)],
        [exchange(s2.at[1], r2.at[1], A2B)],
    ]
    ex3 = [
        [exchange(s3.at[0], r3.at[0], A3)],
        [exchange(s3.at[1], r3.at[1], A3B + ct, lanes_of(ct, 128)) for ct in range(3)],
    ]
    ex4 = [exchange(s4, r4, A4 + ct, lanes_of(ct)) for ct in range(3)]

    def over_dp(sbuf, rbuf, index, same=False):
        return Ring(sbuf, rbuf, ssem.at[index], rsem.at[index], me_d, ND, lambda to: {"dp": to}, same)

    gs_sum, gs_all = over_dp(gss, gsr, GS), over_dp(gsa, gsa, GS + 1, True)
    gf_sum, gf_all = over_dp(gfs, gfr, GF), over_dp(gfa, gfa, GF + 1, True)
    pieces = ((cs_d, cr_d, ys_d, yr_d, xs_d, xr_d), (cs_u, cr_u, ys_u, yr_u, xs_u, xr_u), (cs_l, cr_l, ys_l, yr_l, xs_l, xr_l))
    mate, beside = {"seq": hz * NC + 1 - core}, {"dp": yy * NXL + 1 - xl}
    to_core = [remote(p[0].at[1 - core], p[1], ssem.at[CORE + i], rsem.at[CORE + i], mate) for i, p in enumerate(pieces)]
    to_y = [
        Ring(p[2], p[3], ssem.at[YY + i], rsem.at[YY + i], yy, NY, lambda to: {"dp": to * NXL + xl})
        for i, p in enumerate(pieces)
    ]
    to_x = [remote(p[4].at[1 - xl], p[5], ssem.at[XX + i], rsem.at[XX + i], beside) for i, p in enumerate(pieces)]
    to_last = [
        Ring(a, b, ssem.at[LAST + i], rsem.at[LAST + i], hz, NXH * NZ, lambda to: {"seq": to * NC + core})
        for i, (a, b) in enumerate(((fs, fr), (fsl, frl)))
    ]

    def after_core(i):
        sent, got, ys = pieces[i][:3]
        to_core[i].wait_recv()
        for n in range(NY):
            ys[n] = (sent[core, n].astype(F32) + got[n].astype(F32)).astype(BF16)
        to_y[i].start()

    def after_y(i):
        xs = pieces[i][4]
        to_y[i].recv()
        total = to_y[i].total()
        for h in range(NXL):
            xs[h] = (total[:, 384 * h : 384 * h + 384] if i == 1 else total[48 * h : 48 * h + 48]).astype(BF16)
        to_x[i].start()

    def after_x(i):
        xs, xr = pieces[i][4:]
        to_x[i].wait_recv()
        return (xs[xl].astype(F32) + xr[...].astype(F32)).astype(BF16)

    inward = {}
    for index, (name, source, target) in enumerate((
        ("x", x_hbm, x_ref), ("vw", vw_hbm, vw_ref), ("fb", fb_hbm, fb_ref), ("gw", gw_hbm, gw_ref), ("sb", sb_hbm, sb_ref),
        ("pm", pm_hbm, pm_ref), ("ex", ex_hbm, ex_ref), ("cot", cot_hbm, cot_ref), ("dn", dn_hbm, dn_ref),
        ("ow", ow_hbm, ow_ref), ("up", up_hbm, up_ref), ("p3", p3_hbm, p3_ref), ("p12", p12_hbm, p12_ref),
        ("fold", fold_hbm, fold_ref), ("ufold", ufold_hbm, ufold_ref),
    )):
        inward[name] = pltpu.make_async_copy(source, target, lsem.at[index])
        inward[name].start()
    outward = [pltpu.make_async_copy(out_ref, out_hbm, lsem.at[15])] + [
        pltpu.make_async_copy(
            gin_ref.at[pl.ds(HALF * ii, HALF)], gin_hbm.at[pl.ds(HALF * ii, HALF)], lsem.at[16 + ii]
        )
        for ii in range(2)
    ]

    def loaded(*names):
        for name in names:
            inward[name].wait()

    g1, g2 = g1_ref[...].reshape(1, D), g2_ref[...].reshape(1, D)

    def norm_first(rows, t):
        v = x_ref[rows, :].astype(F32)
        n1[rows, :] = (v * factor_of(v) * g1).astype(BF16)

    loaded("x")
    tiles(ROWS, 32, norm_first)
    loaded("vw", "fb")
    for n in range(NB):
        val[:, blk(n)] = dot(n1[:, blk(n)], vw_ref[:, blk(n)]).astype(BF16)
    for ct in range(3):
        lanes = lanes_of(ct)
        pair = [dot(fb_ref[ii], val[ii * HALF : (ii + 1) * HALF, lanes]) for ii in range(2)]
        s1[:, :, lanes] = pack_pair(*pair)
        if ct == 0:
            all_here()
        ex1[ct].start()

    loaded("sb", "pm", "ex")
    spread = dot(pm_ref[...], sb_ref[...]).astype(BF16)
    for ii in range(2):
        wide = dot(spread[ii * HALF : (ii + 1) * HALF], ex_ref[...])
        mm[ii] = jnp.where(same_block(wide.shape), wide, 0.0).astype(BF16)
    loaded("gw")
    for n in range(NB):
        gate[:, blk(n)] = dot(n1[:, blk(n)], gw_ref[:, blk(n)]).astype(BF16)
    loaded("cot", "dn")
    for n in range(NB):
        for ii in range(2):
            dact[ii, n] = dot(cot_ref[ii * HALF : (ii + 1) * HALF, blk(n)], dn_ref[:, blk(n)], 1, 1)

    for ct in range(3):
        ex1[ct].recv()
        lanes = lanes_of(ct)
        for ii in range(2):
            o = dot(mm[ii], r1[:, :, lanes].reshape(NS * 16, 256))
            s2[ii, :, :, 128 * ct : 128 * ct + 128] = pack_pair(o[:, :128], o[:, 128:])
            if ii == 0:
                ex2[0][ct].start()
    ex2[1][0].start()
    loaded("ow", "up")
    gain2[...] = jnp.zeros_like(gain2)

    def token_half(ii):
        base = ii * HALF
        half = slice(base, base + HALF)

        def rows_of(rows):
            return pl.ds(pl.multiple_of(base + rows.start, rows.size), rows.size)

        for part in ex2[ii]:
            part.recv()

        def gated(rows, t):
            part = r2[ii, pl.ds(pl.multiple_of(t * 4, 4), 4)]

            def store(lane, v):
                at = (rows_of(rows), slice(lane, lane + 128))
                mixed[at] = v.astype(BF16)
                y[at] = (v * gate[at].astype(F32)).astype(BF16)

            unpack_lanes(part, store)

        tiles(HALF, 32, gated)
        for n in range(NB):
            t768[:, blk(n)] = dot(y[half, blk(n)], ow_ref[:, blk(n)])

        def norm_second(rows, t):
            m = (x_ref[rows_of(rows), :].astype(F32) + t768[rows, :]).astype(BF16)
            mid[rows_of(rows), :] = m
            mf = m.astype(F32)
            n2[rows_of(rows), :] = (mf * factor_of(mf) * g2).astype(BF16)

        tiles(HALF, 32, norm_second)
        for n in range(NB):
            hbuf[...] = dot(n2[half, blk(n)], up_ref[:, blk(n, HB)])

            def gelu(rows, t):
                for lt in range(3):
                    lanes = slice(256 * lt, 256 * lt + 256)
                    wide = slice(n * HB + 256 * lt, n * HB + 256 * lt + 256)
                    value, slope = gelu_pair(hbuf[rows, lanes])
                    act[rows_of(rows), wide] = value.astype(BF16)
                    dpre[rows_of(rows), wide] = (slope * dact[ii, n, rows, lanes]).astype(BF16)

            tiles(HALF, 32, gelu)
            t768[:, blk(n)] = dot(dpre[half, blk(n, HB)], up_ref[:, blk(n, HB)], 1, 1)

        def norm_back_second(rows, t):
            mf = mid[rows_of(rows), :].astype(F32)
            f2 = factor_of(mf)
            u2 = mf * f2
            h2 = t768[rows, :]
            gain2[...] = fold_rows(h2 * u2, gain2[...])
            s = h2 * g2
            d = cot_ref[rows_of(rows), :].astype(F32) + f2 * (s - u2 * jnp.mean(s * u2, axis=-1, keepdims=True))
            dmid[rows_of(rows), :] = d.astype(BF16)

        tiles(HALF, 32, norm_back_second)
        for n in range(NB):
            t768[:, blk(n)] = dot(dmid[half, blk(n)], ow_ref[:, blk(n)], 1, 1)

        def gates_back(rows, t):
            dy = t768[rows, :]
            at = rows_of(rows)
            dgate[at, :] = (dy * mixed[at, :].astype(F32)).astype(BF16)
            dm = dy * gate[at, :].astype(F32)
            for ct in range(3):
                low, high = dm[:, 256 * ct : 256 * ct + 128], dm[:, 256 * ct + 128 : 256 * ct + 256]
                s3[ii, pl.ds(pl.multiple_of(t * 4, 4), 4), :, 128 * ct : 128 * ct + 128] = pack_pair(low, high)

        tiles(HALF, 32, gates_back)
        for part in ex3[ii]:
            part.start()

    token_half(0)
    token_half(1)

    loaded("p3", "p12")
    gain2_t = gain2[...].T
    inv_t = jnp.broadcast_to(1.0 / g1, (8, D)).T
    for n in range(NB):
        tmp[:, 0:D] = dot(cot_ref[:, blk(n)], act[:, blk(n, HB)], 0, 0).astype(BF16)
        tmp[:, D : D + DB] = dot(dgate[:, blk(n)], n1[:, blk(n)], 0, 0).astype(BF16)
        tmp[:, D + DB : GL] = dot(dmid[:, blk(n)], y[:, blk(n)], 0, 0).astype(BF16)
        tmp[:, GL:DL] = jnp.concatenate([gain2_t[blk(n)], jnp.zeros((DB, 120), F32)], axis=1).astype(BF16)
        moved = dot(p3_ref[...], tmp[...]).astype(BF16)
        cs_d[0, n] = moved[:96]
        cs_d[1, n] = moved[96:]
    to_core[0].start()

    def unpack_mixed(ii, ct):
        def step(rows, t):
            v = r3[ii, pl.ds(pl.multiple_of(t * 4, 4), 4), :, 128 * ct : 128 * ct + 128].astype(F32).reshape(4, 2, 8, 128)
            at = pl.ds(pl.multiple_of(ii * HALF + t * 32, 32), 32)
            for h in range(2):
                lane = 256 * ct + 128 * h
                dmu[at, lane : lane + 128] = v[:, h].reshape(32, 128).astype(BF16)

        tiles(HALF, 32, step)

    def second_back(ct):
        if ct == 0:
            ex3[0][0].recv()
            for every in range(3):
                unpack_mixed(0, every)
        ex3[1][ct].recv()
        unpack_mixed(1, ct)
        lanes = lanes_of(ct)
        s4[:, :, lanes] = dot(mm[...].reshape(ROWS, ROWS), dmu[:, lanes], 0, 0).astype(BF16).reshape(NS, 16, 256)
        ex4[ct].start()

    second_back(0)
    for n in range(NB):
        grad_up = dot(dpre[:, blk(n, HB)], n2[:, blk(n)], 0, 0).astype(BF16)
        for q in range(4):
            moved = dot(p12_ref[...], grad_up[blk(q)]).astype(BF16)
            cs_u[0, n, :, blk(q)] = moved[:96]
            cs_u[1, n, :, blk(q)] = moved[96:]
    to_core[1].start()
    second_back(1)
    after_core(0)
    second_back(2)
    after_core(1)

    for ii in range(2):
        g = dot(dmu[ii * HALF : (ii + 1) * HALF, :], r1[...].reshape(ROWS, D), 1, 1) * MIX_SCALE
        g = dot(jnp.where(same_block(g.shape), g, 0.0).astype(BF16), ex_ref[...], 1, 1)
        gsec[:, 64 * ii : 64 * ii + 64] = g.astype(BF16)
    for part in range(ND):
        gss[part] = gsec[32 * part : 32 * part + 32, :]
    gs_sum.start()

    for n in range(NB):
        t = dot(act[:, blk(n, HB)], dn_ref[:, blk(n)])
        out_ref[:, blk(n)] = (mid[:, blk(n)].astype(F32) + t).astype(BF16)
    outward[0].start()
    for n in range(NB):
        h1g[:, blk(n)] = dot(dgate[:, blk(n)], gw_ref[:, blk(n)], 1, 1)
        g = dot(n1[:, blk(n)], dgate[:, blk(n)], 0, 0) * gw_ref[:, blk(n)].astype(F32)
        gcol[blk(n), :] = jnp.broadcast_to(jnp.sum(g, axis=-1, keepdims=True), (DB, 8))
    gs_sum.recv()
    gsa[me_d] = gs_sum.total().astype(BF16)
    gs_all.start()
    after_y(0)
    after_y(1)

    for ct in range(3):
        ex4[ct].recv()
        lanes = lanes_of(ct)
        v = r4[:, :, lanes].astype(F32).reshape(NS, 2, 8, 256)
        for ii in range(2):
            half = slice(ii * HALF, (ii + 1) * HALF)
            df[half, lanes] = v[:, ii].reshape(HALF, 256).astype(BF16)
            g = dot(df[half, lanes], val[half, lanes], 1, 1)
            gfull[ii] = g if ct == 0 else gfull[ii] + g
            if ct == 2:
                for part in range(4):
                    gfs[4 * ii + part] = (gfull[ii, 64 * part : 64 * part + 64, :] * MIX_SCALE).astype(BF16)
        if ct == 2:
            gf_sum.start()
        for ii in range(2):
            half = slice(ii * HALF, (ii + 1) * HALF)
            dval[half, lanes] = dot(fb_ref[ii], df[half, lanes], 0, 0).astype(BF16)

    for n in range(NB):
        grad_v = dot(dval[:, blk(n)], n1[:, blk(n)], 0, 0)
        g = dot(n1[:, blk(n)], dval[:, blk(n)], 0, 0) * vw_ref[:, blk(n)].astype(F32)
        g = (jnp.sum(g, axis=-1, keepdims=True) + gcol[blk(n), 0:1]) * inv_t[blk(n), 0:1]
        column = jnp.where(lax.broadcasted_iota(jnp.int32, (DB, 64), 1) == 0, g, 0.0)
        moved = dot(p3_ref[...], jnp.concatenate([grad_v, column], axis=1).astype(BF16)).astype(BF16)
        cs_l[0, n] = moved[:96]
        cs_l[1, n] = moved[96:]
    to_core[2].start()

    loaded("fold", "ufold")
    dd, uu = after_x(0), after_x(1)
    folded = dot(fold_ref[:, 0:48], dd[:, 0:512]) + dot(fold_ref[:, 48:96], dd[:, 512:1024])
    fs[:, :, :] = folded.astype(BF16).reshape(16, 16, 512)
    tail = dot(fold_ref[:, 96:144], dd[:, 1024:1280]).astype(BF16).reshape(16, 16, 256)
    fs[:, :, 0:256] = fs[:, :, 0:256] + tail
    for h in range(NXH):
        u = uu[:, DB * h : DB * h + DB]
        low = dot(ufold_ref[:, 0:96], u).astype(BF16).reshape(8, 16, DB)
        high = dot(ufold_ref[:, 96:192], u).astype(BF16).reshape(8, 16, DB)
        at = slice(8 * h, 8 * h + 8)
        fs[at, :, 0:DB] = fs[at, :, 0:DB] + low
        fs[at, :, 256 : 256 + DB] = fs[at, :, 256 : 256 + DB] + high
    to_last[0].start()
    after_core(2)

    def input_gradient(ii):
        half = slice(ii * HALF, (ii + 1) * HALF)
        for n in range(NB):
            t768[:, blk(n)] = dot(dval[half, blk(n)], vw_ref[:, blk(n)], 1, 1)

        def norm_back_first(rows, t):
            at = pl.ds(pl.multiple_of(ii * HALF + t * 32, 32), 32)
            v = x_ref[at, :].astype(F32)
            f1 = factor_of(v)
            u1 = v * f1
            s = (t768[rows, :] + h1g[at, :]) * g1
            d = dmid[at, :].astype(F32) + f1 * (s - u1 * jnp.mean(s * u1, axis=-1, keepdims=True))
            gin_ref[at, :] = d.astype(BF16)

        tiles(HALF, 32, norm_back_first)
        outward[1 + ii].start()

    input_gradient(0)
    gf_sum.recv()
    gfa[me_d] = gf_sum.total().astype(BF16)
    gf_all.start()
    after_y(2)
    input_gradient(1)
    ll = after_x(2)
    folded = dot(fold_ref[:, 0:48], ll[:, 0:128]) + dot(fold_ref[:, 48:96], ll[:, 128:256])
    fsl[...] = folded.astype(BF16).reshape(16, 16, 128)
    to_last[1].start()

    to_last[0].recv()
    early_ref[...] = to_last[0].total()
    gs_all.recv()
    gf_all.recv()
    for part in range(ND):
        mix_ref[64 * part : 64 * part + 64, :] = gfa[part]
        mix_ref[512 + 16 * part : 528 + 16 * part, 0:128] = gsa[part, 0:16]
        mix_ref[512 + 16 * part : 528 + 16 * part, 128:256] = gsa[part, 16:32]
    to_last[1].recv()
    late_ref[...] = to_last[1].total()

    for part in ex1 + ex2[0] + ex2[1] + ex3[0] + ex3[1] + ex4 + [gs_sum, gs_all, gf_sum, gf_all] + to_y + to_last:
        part.sent()
    for copy in to_core + to_x:
        copy.wait_send()
    for copy in outward:
        copy.wait()


def finish_kernel(
    out_in, gin_in, mix_ref, early_ref, late_ref, pm_ref,
    out_ref, gin_ref, gv_ref, gg_ref, go_ref, gu_ref, gd_ref, g1_ref, g2_ref, gfirst_ref, gsecond_ref,
    spread, sem,
):
    copies = [pltpu.make_async_copy(out_in, out_ref, sem.at[0]), pltpu.make_async_copy(gin_in, gin_ref, sem.at[1])]
    for copy in copies:
        copy.start()
    for part in range(ND):
        at = 64 * (part % 4)
        gfirst_ref[part // 4, at : at + 64, :] = mix_ref[64 * part : 64 * part + 64, :].astype(F32)
        spread[32 * part : 32 * part + 16, :] = mix_ref[512 + 16 * part : 528 + 16 * part, 0:128]
        spread[32 * part + 16 : 32 * part + 32, :] = mix_ref[512 + 16 * part : 528 + 16 * part, 128:256]
    gsecond_ref[...] = dot(pm_ref[0:HALF, :], spread[:, 0:64], 0, 0) + dot(pm_ref[HALF:ROWS, :], spread[:, 64:128], 0, 0)
    total, late = early_ref[...] * ROW_SCALE, late_ref[...] * ROW_SCALE
    gd_ref[:, 0:512] = total[0:3]
    gd_ref[:, 512:768] = total[3:6, 0:256]
    gg_ref[...] = total[3:6, 256:448]
    go_ref[:, 0:64] = total[3:6, 448:512]
    go_ref[:, 64:192] = total[6:9, 0:128]
    gu_ref[0:6, :] = total[9:15, 0:192]
    gu_ref[6:12, :] = total[9:15, 256:448]
    gv_ref[:, 0:128] = late[0:3]
    gv_ref[:, 128:192] = late[3:6, 0:64]

    def across(column):
        square = lax.broadcasted_iota(jnp.int32, (8, 128), 0) == lax.broadcasted_iota(jnp.int32, (8, 128), 1)
        return jnp.sum(jnp.where(square, column, 0.0), axis=0, keepdims=True)[:, 0:3]

    pad = jnp.zeros((5, 1), F32)
    g2_ref[...] = across(jnp.concatenate([jnp.sum(total[6:9, 128:136], axis=1, keepdims=True), pad], axis=0))
    g1_ref[...] = across(jnp.concatenate([late[3:6, 64:65], pad], axis=0))
    for copy in copies:
        copy.wait()


def vmem_specs(count):
    return [pl.BlockSpec(memory_space=pltpu.VMEM)] * count


def any_specs(count):
    return [pl.BlockSpec(memory_space=pl.ANY)] * count


def body(inputs, cotangent, gain_first, gain_second, value_w, gate_w, out_w, up_w, down_w, first_blocks, second_blocks):
    perm_m, expand, perm3, perm12, fold, ufold = [jnp.asarray(a, BF16) for a in constants()]
    shape = jax.ShapeDtypeStruct
    vm = lambda *s: pltpu.VMEM(s, BF16)
    vf = lambda *s: pltpu.VMEM(s, F32)
    big = lambda: vm(ROWS, D)
    dma = pltpu.SemaphoreType.DMA
    out, gin, mix, early, late = pl.pallas_call(
        main_kernel,
        out_shape=[
            shape((ROWS, D), BF16), shape((ROWS, D), BF16), shape((640, 256), BF16), shape((16, 512), F32),
            shape((16, 128), F32),
        ],
        in_specs=any_specs(2) + vmem_specs(2) + any_specs(13),
        out_specs=any_specs(2) + vmem_specs(3),
        scratch_shapes=[
            big(), big(), vm(DB, D), vm(DB, D), vm(DB, D), vm(DB, NB * HB), vm(D, D), vm(2, 256, 256), vm(512, 64),
            vm(512, 512), vm(64, 512), vm(192, 192), vm(192, 192), vm(256, 144), vm(128, 192), big(), big(),
            big(), big(), big(), big(), big(), big(), big(), big(), big(), big(), big(),
            vm(ROWS, NB * HB), vm(ROWS, NB * HB), vf(2, NB, HALF, HB),
            vm(2, HALF, ROWS), big(), vf(HALF, D), vf(HALF, HB), vf(ROWS, D), vf(2, 256, 256),
            vm(NS, 16, D), vm(NS, 16, D), vm(2, NS, 16, 384), vm(2, NS, 16, 384),
            vm(2, NS, 16, 384), vm(2, NS, 16, 384), vm(NS, 16, D), vm(NS, 16, D),
            vm(ND, 32, 128), vm(ND, 32, 128), vm(ND, 32, 128), vm(ND, 64, 256), vm(ND, 64, 256), vm(ND, 64, 256),
            vm(HALF, 128), vf(8, D), vf(D, 8), vm(DB, DL),
            vm(2, NB, 96, DL), vm(2, NB, 96, UL), vm(2, NB, 96, LW), vm(NB, 96, DL), vm(NB, 96, UL), vm(NB, 96, LW),
            vm(NY, 96, DL), vm(NY, 96, UL), vm(NY, 96, LW), vm(NY, 96, DL), vm(NY, 96, UL), vm(NY, 96, LW),
            vm(2, 48, DL), vm(2, 96, 384), vm(2, 48, LW), vm(48, DL), vm(96, 384), vm(48, LW),
            vm(16, 16, 512), vm(16, 16, 512), vm(16, 16, 128), vm(16, 16, 128),
            dma((SEMS,)), dma((SEMS,)), dma((18,)),
        ],
        compiler_params=pltpu.CompilerParams(
            collective_id=0, has_side_effects=True, vmem_limit_bytes=VMEM_LIMIT
        ),
    )(
        inputs.reshape(ROWS, D), cotangent.reshape(ROWS, D), gain_first, gain_second,
        value_w, gate_w, out_w, up_w, down_w, first_blocks, second_blocks.reshape(512, 64),
        perm_m, expand, perm3, perm12, fold, ufold,
    )
    out, gin, gv, gg, go, gu, gd, g1, g2, gfirst, gsecond = pl.pallas_call(
        finish_kernel,
        out_shape=[
            shape((ROWS, D), BF16), shape((ROWS, D), BF16), shape((3, DB), F32), shape((3, DB), F32), shape((3, DB), F32),
            shape((12, DB), F32), shape((3, HB), F32), shape((1, 3), F32), shape((1, 3), F32), shape((2, 256, 256), F32),
            shape((512, 64), F32),
        ],
        in_specs=any_specs(2) + vmem_specs(4),
        out_specs=vmem_specs(11),
        scratch_shapes=[vm(HALF, 128), dma((2,))],
    )(out, gin, mix, early, late, perm_m)
    return (
        out.reshape(1, ROWS, D), gin.reshape(1, ROWS, D), gv.T, gg.T, go.T, gu.T, gd.T, g1.reshape(3), g2.reshape(3),
        gfirst, gsecond.reshape(8, 64, 64),
    )


def solution(mesh):
    tokens, whole = P("dp", "seq", None), P("seq", None, None)
    columns = P(None, ("dp", "seq"))
    gains = P(("dp", "seq"))
    return jax.shard_map(
        body,
        mesh=mesh,
        in_specs=(tokens, tokens, P(), P(), P(), P(), P(), P(), P(), whole, whole),
        out_specs=(tokens, tokens, columns, columns, columns, columns, columns, gains, gains, whole, whole),
        check_vma=False,
    )
```

```python
import functools
import math

import jax
import jax.numpy as jnp
import numpy as np
from jax import lax
from jax.experimental import pallas as pl
from jax.experimental.pallas import tpu as pltpu
from jax.sharding import PartitionSpec as P

MESH = pl.DeviceIdType.MESH
F32 = jnp.float32
BF16 = jnp.bfloat16
EPS = 1e-6
NY, NXL, NXH, NZ, NC = 4, 2, 2, 8, 2
NS, ND = NXH * NZ * NC, NY * NXL
D, NB, DB, HB, ROWS, HALF = 768, 4, 192, 768, 512, 256
ROW_SCALE = 1.0 / math.sqrt(131072.0)
MIX_SCALE = 1.0 / math.sqrt(6144.0)
DL, UL, LW = 1152, 768, 256
A1, A2, A2B, A3, A3B, A4, GS, GF, CORE, YY, XX, LAST = 0, 3, 6, 7, 8, 11, 15, 17, 21, 33, 36, 38
SEMS = 40
VMEM_LIMIT = 60 * 2**20


def dot(a, b, ca=1, cb=0):
    return lax.dot_general(a, b, (((ca,), (cb,)), ((), ())), preferred_element_type=F32)


def constants():
    one = lambda shape, pairs: _onehot(shape, pairs)
    row, col = [], []
    for ii in range(2):
        for d in range(NS):
            for bl in range(8):
                row.append(ii * 256 + d * 8 + bl)
                col.append(bl * 64 + 2 * d + ii)
    perm_m = one((512, 512), (row, col))
    expand = one((64, 512), (np.arange(512) // 8, np.arange(512)))
    out = np.arange(192)
    c, rem = out // 96, out % 96
    perm3 = one((192, 192), (out, rem // 3 * 6 + c * 3 + rem % 3))
    perm12 = one((192, 192), (out, rem // 12 * 24 + c * 12 + rem % 12))
    dest, t = np.arange(48) // 3, np.arange(48) % 3
    fold = np.concatenate([one((256, 48), (dest * 16 + 3 * f + t, np.arange(48))) for f in range(3)], axis=1)
    z, t = np.arange(96) // 12, np.arange(96) % 12
    low, high = t < 6, t >= 6
    ufold = np.concatenate(
        [
            one((128, 96), ((z * 16 + 9 + t)[low], np.arange(96)[low])),
            one((128, 96), ((z * 16 + 3 + t)[high], np.arange(96)[high])),
        ],
        axis=1,
    )
    return perm_m, expand, perm3, perm12, fold, ufold


def _onehot(shape, pairs):
    array = np.zeros(shape, np.float32)
    array[pairs[0], pairs[1]] = 1.0
    return array


def remote(src, dst, ssem, rsem, device):
    return pltpu.make_async_remote_copy(
        src_ref=src, dst_ref=dst, send_sem=ssem, recv_sem=rsem, device_id=device, device_id_type=MESH
    )


def seq_peer(k, me):
    g, t = k // 8, k % 8
    dx, dc = 1 - g // 2, ((g + 1) // 2) % 2
    dz = 4 + (1 - 2 * (t % 2)) * ((t + 1) // 2)
    xh, z, c = me // 16, (me // 2) % 8, me % 2
    return ((xh + dx) % 2) * 16 + ((z + dz) % 8) * 2 + (c + dc) % 2


def greet(me_s, me_d):
    barrier = pltpu.get_barrier_semaphore()

    def over_seq(k, carry):
        pl.semaphore_signal(barrier, inc=1, device_id={"seq": seq_peer(k, me_s)}, device_id_type=MESH)
        return carry

    def over_dp(k, carry):
        pl.semaphore_signal(barrier, inc=1, device_id={"dp": lax.rem(me_d + k, ND)}, device_id_type=MESH)
        return carry

    lax.fori_loop(0, NS - 1, over_seq, 0)
    lax.fori_loop(1, ND, over_dp, 0)
    return lambda: pl.semaphore_wait(barrier, NS - 1 + ND - 1)


class Exchange:
    def __init__(self, sbuf, rbuf, ssem, rsem, me, lanes=None):
        self.me, self.sems = me, (ssem, rsem)
        self.sbuf, self.rbuf, self.lanes = sbuf, rbuf, lanes

    def at(self, ref, index):
        return ref.at[index] if self.lanes is None else ref.at[index, :, self.lanes]

    def start(self):
        def send(k, carry):
            peer = seq_peer(k, self.me)
            remote(self.at(self.sbuf, peer), self.at(self.rbuf, self.me), *self.sems, {"seq": peer}).start()
            return carry

        lax.fori_loop(0, NS - 1, send, 0)
        if self.lanes is None:
            self.rbuf[self.me] = self.sbuf[self.me]
        else:
            self.rbuf[self.me, :, self.lanes] = self.sbuf[self.me, :, self.lanes]

    def whole(self):
        part = pl.ds(0, NS - 1)
        return remote(self.at(self.sbuf, part), self.at(self.rbuf, part), *self.sems, {"seq": self.me})

    def recv(self):
        self.whole().wait_recv()

    def sent(self):
        self.whole().wait_send()


class Ring:
    def __init__(self, sbuf, rbuf, ssem, rsem, me, count, device, same=False):
        self.sbuf, self.rbuf, self.sems = sbuf, rbuf, (ssem, rsem)
        self.me, self.count, self.device, self.same = me, count, device, same

    def one(self, to):
        remote(self.sbuf.at[to], self.rbuf.at[self.me], *self.sems, self.device(to)).start()

    def own(self, to):
        self.rbuf[to] = self.sbuf[to]

    def start(self):
        def send(k, carry):
            to = lax.rem(self.me + k, self.count)
            source = self.sbuf.at[self.me if self.same else to]
            remote(source, self.rbuf.at[self.me], *self.sems, self.device(to)).start()
            return carry

        lax.fori_loop(1, self.count, send, 0)
        if not self.same:
            self.rbuf[self.me] = self.sbuf[self.me]

    def whole(self):
        part = pl.ds(0, self.count - 1)
        return remote(self.sbuf.at[part], self.rbuf.at[part], *self.sems, self.device(self.me))

    def recv(self):
        self.whole().wait_recv()

    def sent(self):
        self.whole().wait_send()

    def total(self):
        out = self.rbuf[0].astype(F32)
        for k in range(1, self.count):
            out = out + self.rbuf[k].astype(F32)
        return out


def tiles(rows, tile, body):
    def step(t, carry):
        body(pl.ds(pl.multiple_of(t * tile, tile), tile), t)
        return carry

    lax.fori_loop(0, rows // tile, step, 0)


def blk(n, width=DB):
    return slice(n * width, (n + 1) * width)


def unpack_lanes(packed, store):
    count = packed.shape[0]
    for t in range(3):
        v = packed[:, :, 128 * t : 128 * t + 128].astype(F32).reshape(count, 2, 8, 128)
        store(256 * t, v[:, 0].reshape(count * 8, 128))
        store(256 * t + 128, v[:, 1].reshape(count * 8, 128))


def pack_pair(low, high):
    count = low.shape[0] // 8
    both = jnp.concatenate([low.reshape(count, 8, -1), high.reshape(count, 8, -1)], axis=1)
    return both.astype(BF16)


def factor_of(rows):
    return lax.rsqrt(jnp.mean(rows * rows, axis=-1, keepdims=True) + EPS)


def gelu_pair(h):
    size = jnp.abs(h)
    den = 1.0 + (0.3275911 / math.sqrt(2.0)) * size
    t = pl.reciprocal(den, approx=True)
    t = t * (2.0 - den * t)
    e = jnp.exp(-0.5 * (h * h))
    poly = 0.5 * 1.061405429
    for a in (-1.453152027, 1.421413741, -0.284496736, 0.254829592):
        poly = poly * t + 0.5 * a
    q = poly * t * e
    cdf = jnp.where(h >= 0.0, 1.0 - q, q)
    return h * cdf, cdf + h * (e * (1.0 / math.sqrt(2.0 * math.pi)))


def same_block(shape):
    return (lax.broadcasted_iota(jnp.int32, shape, 0) & 7) == (lax.broadcasted_iota(jnp.int32, shape, 1) & 7)


def main_kernel(
    x_hbm, cot_hbm, g1_ref, g2_ref, vw_hbm, gw_hbm, ow_hbm, up_hbm, dn_hbm, fb_hbm, sb_hbm,
    pm_hbm, ex_hbm, p3_hbm, p12_hbm, fold_hbm, ufold_hbm,
    out_hbm, gin_hbm, mix_ref, early_ref, late_ref,
    x_ref, cot_ref, vw_ref, gw_ref, ow_ref, up_ref, dn_ref, fb_ref, sb_ref,
    pm_ref, ex_ref, p3_ref, p12_ref, fold_ref, ufold_ref, out_ref, gin_ref,
    n1, val, gate, mixed, y, mid, n2, dmid, dgate, df, dval, act, dpre, dact, mm, dmu, t768, hbuf, h1g,
    s1, r1, s2, r2, s3, r3, s4, r4, gss, gsr, gsa, gfs, gfr, gfa, gsec, gcol, gcol2, tmp,
    cs_d, cs_u, cs_l, cr_d, cr_u, cr_l, ys_d, ys_u, ys_l, yr_d, yr_u, yr_l,
    xs_d, xs_u, xr_d, xr_u, fs, fr, fsl, frl,
    ssem, rsem, lsem,
):
    me_s, me_d = lax.axis_index("seq"), lax.axis_index("dp")
    yy, xl = me_d // NXL, lax.rem(me_d, NXL)
    hz, core = me_s // NC, lax.rem(me_s, NC)
    all_here = greet(me_s, me_d)

    def exchange(sbuf, rbuf, index, lanes=None):
        return Exchange(sbuf, rbuf, ssem.at[index], rsem.at[index], me_s, lanes)

    def lanes_of(ct, width=256):
        return slice(width * ct, width * ct + width)

    ex1 = [exchange(s1, r1, A1 + ct, lanes_of(ct)) for ct in range(3)]
    ex2 = [
        [exchange(s2.at[0], r2.at[0], A2 + ct, lanes_of(ct, 128)) for ct in range(3)],
        [exchange(s2.at[1], r2.at[1], A2B)],
    ]
    ex3 = [
        [exchange(s3.at[0], r3.at[0], A3)],
        [exchange(s3.at[1], r3.at[1], A3B + ct, lanes_of(ct, 128)) for ct in range(3)],
    ]
    ex4 = [exchange(s4.at[0], r4.at[0], A4 + ct, lanes_of(ct, 128)) for ct in range(3)] + [exchange(s4.at[1], r4.at[1], A4 + 3)]

    def over_dp(sbuf, rbuf, index, same=False):
        return Ring(sbuf, rbuf, ssem.at[index], rsem.at[index], me_d, ND, lambda to: {"dp": to}, same)

    gs_sum, gs_all = over_dp(gss, gsr, GS), over_dp(gsa, gsa, GS + 1, True)
    gf_sum = [over_dp(gfs.at[ii], gfr.at[ii], GF + ii) for ii in range(2)]
    gf_all = [over_dp(gfa.at[ii], gfa.at[ii], GF + 2 + ii, True) for ii in range(2)]
    pieces = ((cs_d, cr_d, ys_d, yr_d, xs_d, xr_d), (cs_u, cr_u, ys_u, yr_u, xs_u, xr_u), (cs_l, cr_l, ys_l, yr_l))
    mate, beside = {"seq": hz * NC + 1 - core}, {"dp": yy * NXL + 1 - xl}
    to_core = [
        [
            remote(p[0].at[1 - core, n], p[1].at[n], ssem.at[CORE + 4 * i + n], rsem.at[CORE + 4 * i + n], mate)
            for n in range(NY)
        ]
        for i, p in enumerate(pieces)
    ]
    to_y = [
        Ring(p[2], p[3], ssem.at[YY + i], rsem.at[YY + i], yy, NY, lambda to: {"dp": to * NXL + xl})
        for i, p in enumerate(pieces[:2])
    ] + [over_dp(ys_l, yr_l, YY + 2)]
    to_x = [remote(p[4].at[1 - xl], p[5], ssem.at[XX + i], rsem.at[XX + i], beside) for i, p in enumerate(pieces[:2])]
    to_last = [
        Ring(a, b, ssem.at[LAST + i], rsem.at[LAST + i], hz, NXH * NZ, lambda to: {"seq": to * NC + core})
        for i, (a, b) in enumerate(((fs, fr), (fsl, frl)))
    ]

    def after_core(i, n):
        sent, got, ys = pieces[i][:3]
        to_core[i][n].wait_recv()
        both = (sent[core, n].astype(F32) + got[n].astype(F32)).astype(BF16)
        if i == 2:
            for h in range(NXL):
                ys[NXL * n + h] = both[48 * h : 48 * h + 48]
            if n == NY - 1:
                to_y[2].start()
        else:
            ys[n] = both

            @pl.when(yy != n)
            def _():
                to_y[i].one(n)

            @pl.when(yy == n)
            def _():
                to_y[i].own(n)

    def after_y(i):
        xs = pieces[i][4]
        to_y[i].recv()
        total = to_y[i].total()
        for h in range(NXL):
            xs[h] = (total[:, 384 * h : 384 * h + 384] if i == 1 else total[48 * h : 48 * h + 48]).astype(BF16)
        to_x[i].start()

    def after_x(i):
        xs, xr = pieces[i][4:]
        to_x[i].wait_recv()
        return (xs[xl].astype(F32) + xr[...].astype(F32)).astype(BF16)

    inward = {}
    for index, (name, source, target) in enumerate((
        ("x", x_hbm, x_ref), ("vw", vw_hbm, vw_ref), ("fb", fb_hbm, fb_ref), ("gw", gw_hbm, gw_ref), ("sb", sb_hbm, sb_ref),
        ("pm", pm_hbm, pm_ref), ("ex", ex_hbm, ex_ref), ("cot", cot_hbm, cot_ref), ("dn", dn_hbm, dn_ref),
        ("ow", ow_hbm, ow_ref), ("up", up_hbm, up_ref), ("p3", p3_hbm, p3_ref), ("p12", p12_hbm, p12_ref),
        ("fold", fold_hbm, fold_ref), ("ufold", ufold_hbm, ufold_ref),
    )):
        inward[name] = pltpu.make_async_copy(source, target, lsem.at[index])
        inward[name].start()
    outward = [pltpu.make_async_copy(out_ref, out_hbm, lsem.at[15])] + [
        pltpu.make_async_copy(
            gin_ref.at[pl.ds(HALF * ii, HALF)], gin_hbm.at[pl.ds(HALF * ii, HALF)], lsem.at[16 + ii]
        )
        for ii in range(2)
    ]

    def loaded(*names):
        for name in names:
            inward[name].wait()

    g1, g2 = g1_ref[...].reshape(1, D), g2_ref[...].reshape(1, D)

    def norm_first(rows, t):
        v = x_ref[rows, :].astype(F32)
        n1[rows, :] = (v * factor_of(v) * g1).astype(BF16)

    loaded("x")
    tiles(ROWS, 32, norm_first)
    loaded("vw", "fb")
    for ct in range(3):
        for n in ((0, 1), (2,), (3,))[ct]:
            val[:, blk(n)] = dot(n1[:, blk(n)], vw_ref[:, blk(n)]).astype(BF16)
        lanes = lanes_of(ct)
        pair = [dot(fb_ref[ii], val[ii * HALF : (ii + 1) * HALF, lanes]) for ii in range(2)]
        s1[:, :, lanes] = pack_pair(*pair)
        if ct == 0:
            all_here()
        ex1[ct].start()

    loaded("sb", "pm", "ex")
    spread = dot(pm_ref[...], sb_ref[...]).astype(BF16)
    for ii in range(2):
        wide = dot(spread[ii * HALF : (ii + 1) * HALF], ex_ref[...])
        mm[ii] = jnp.where(same_block(wide.shape), wide, 0.0).astype(BF16)
    loaded("gw")
    for n in range(NB):
        gate[:, blk(n)] = dot(n1[:, blk(n)], gw_ref[:, blk(n)]).astype(BF16)
    loaded("cot", "dn")
    for n in range(NB):
        for ii in range(2):
            dact[ii, n] = dot(cot_ref[ii * HALF : (ii + 1) * HALF, blk(n)], dn_ref[:, blk(n)], 1, 1)

    for ct in range(3):
        ex1[ct].recv()
        lanes = lanes_of(ct)
        for ii in range(2):
            o = dot(mm[ii], r1[:, :, lanes].reshape(NS * 16, 256))
            s2[ii, :, :, 128 * ct : 128 * ct + 128] = pack_pair(o[:, :128], o[:, 128:])
            if ii == 0:
                ex2[0][ct].start()
    ex2[1][0].start()
    loaded("ow", "up")

    def token_half(ii):
        base = ii * HALF
        half = slice(base, base + HALF)

        def rows_of(rows):
            return pl.ds(pl.multiple_of(base + rows.start, rows.size), rows.size)

        for part in ex2[ii]:
            part.recv()

        def gated(rows, t):
            part = r2[ii, pl.ds(pl.multiple_of(t * 4, 4), 4)]

            def store(lane, v):
                at = (rows_of(rows), slice(lane, lane + 128))
                mixed[at] = v.astype(BF16)
                y[at] = (v * gate[at].astype(F32)).astype(BF16)

            unpack_lanes(part, store)

        tiles(HALF, 32, gated)
        for n in range(NB):
            t768[:, blk(n)] = dot(y[half, blk(n)], ow_ref[:, blk(n)])

        def norm_second(rows, t):
            m = (x_ref[rows_of(rows), :].astype(F32) + t768[rows, :]).astype(BF16)
            mid[rows_of(rows), :] = m
            mf = m.astype(F32)
            n2[rows_of(rows), :] = (mf * factor_of(mf) * g2).astype(BF16)

        tiles(HALF, 32, norm_second)
        for n in range(NB):
            hbuf[...] = dot(n2[half, blk(n)], up_ref[:, blk(n, HB)])

            def gelu(rows, t):
                for lt in range(3):
                    lanes = slice(256 * lt, 256 * lt + 256)
                    wide = slice(n * HB + 256 * lt, n * HB + 256 * lt + 256)
                    value, slope = gelu_pair(hbuf[rows, lanes])
                    act[rows_of(rows), wide] = value.astype(BF16)
                    dpre[rows_of(rows), wide] = (slope * dact[ii, n, rows, lanes]).astype(BF16)

            tiles(HALF, 32, gelu)
            t768[:, blk(n)] = dot(dpre[half, blk(n, HB)], up_ref[:, blk(n, HB)], 1, 1)

        def norm_back_second(rows, t):
            mf = mid[rows_of(rows), :].astype(F32)
            f2 = factor_of(mf)
            u2 = mf * f2
            h2 = t768[rows, :]
            s = h2 * g2
            d = cot_ref[rows_of(rows), :].astype(F32) + f2 * (s - u2 * jnp.mean(s * u2, axis=-1, keepdims=True))
            dmid[rows_of(rows), :] = d.astype(BF16)

        tiles(HALF, 32, norm_back_second)
        for n in range(NB):
            t768[:, blk(n)] = dot(dmid[half, blk(n)], ow_ref[:, blk(n)], 1, 1)

        def gates_back(rows, t):
            dy = t768[rows, :]
            at = rows_of(rows)
            dgate[at, :] = (dy * mixed[at, :].astype(F32)).astype(BF16)
            dm = dy * gate[at, :].astype(F32)
            for ct in range(3):
                low, high = dm[:, 256 * ct : 256 * ct + 128], dm[:, 256 * ct + 128 : 256 * ct + 256]
                s3[ii, pl.ds(pl.multiple_of(t * 4, 4), 4), :, 128 * ct : 128 * ct + 128] = pack_pair(low, high)

        tiles(HALF, 32, gates_back)
        for part in ex3[ii]:
            part.start()

    token_half(0)
    token_half(1)

    def unpack_mixed(ii, ct):
        def step(rows, t):
            v = r3[ii, pl.ds(pl.multiple_of(t * 4, 4), 4), :, 128 * ct : 128 * ct + 128].astype(F32).reshape(4, 2, 8, 128)
            at = pl.ds(pl.multiple_of(ii * HALF + t * 32, 32), 32)
            for h in range(2):
                lane = 256 * ct + 128 * h
                dmu[at, lane : lane + 128] = v[:, h].reshape(32, 128).astype(BF16)

        tiles(HALF, 32, step)

    def second_back(ct):
        if ct == 0:
            ex3[0][0].recv()
            for every in range(3):
                unpack_mixed(0, every)
        ex3[1][ct].recv()
        unpack_mixed(1, ct)
        lanes = lanes_of(ct)
        o = dot(mm[...].reshape(ROWS, ROWS), dmu[:, lanes], 0, 0).reshape(NS, 2, 8, 256)
        for ii in range(2):
            low, high = o[:, ii, :, :128].reshape(HALF, 128), o[:, ii, :, 128:].reshape(HALF, 128)
            s4[ii, :, :, 128 * ct : 128 * ct + 128] = pack_pair(low, high)
        ex4[ct].start()
        if ct == 2:
            ex4[3].start()

    loaded("p3", "p12")
    inv1 = jnp.broadcast_to(1.0 / g1, (8, D)).T
    inv2 = jnp.broadcast_to(1.0 / g2, (8, D)).T

    def piece_down(n):
        tmp[:, 0:D] = dot(cot_ref[:, blk(n)], act[:, blk(n, HB)], 0, 0).astype(BF16)
        tmp[:, D : D + DB] = dot(dgate[:, blk(n)], n1[:, blk(n)], 0, 0).astype(BF16)
        tmp[:, D + DB : DL] = dot(dmid[:, blk(n)], y[:, blk(n)], 0, 0).astype(BF16)
        moved = dot(p3_ref[...], tmp[...]).astype(BF16)
        cs_d[0, n] = moved[:96]
        cs_d[1, n] = moved[96:]
        to_core[0][n].start()

    def piece_up(n):
        g = dot(n2[:, blk(n)], dpre[:, blk(n, HB)], 0, 0)
        column = jnp.sum(g * up_ref[:, blk(n, HB)].astype(F32), axis=-1, keepdims=True) * inv2[blk(n), 0:1]
        gcol2[blk(n), :] = jnp.broadcast_to(column, (DB, 8))
        for q in range(4):
            moved = dot(p12_ref[...], g[:, blk(q)].astype(BF16), 1, 1).astype(BF16)
            cs_u[0, n, :, blk(q)] = moved[:96]
            cs_u[1, n, :, blk(q)] = moved[96:]
        to_core[1][n].start()

    piece_down(0)
    piece_down(1)
    after_core(0, 0)
    piece_down(2)
    after_core(0, 1)
    piece_down(3)
    after_core(0, 2)
    second_back(0)
    piece_up(0)
    after_core(0, 3)
    piece_up(1)
    after_core(1, 0)
    second_back(1)
    piece_up(2)
    after_core(1, 1)
    piece_up(3)
    after_core(1, 2)
    second_back(2)
    after_core(1, 3)

    for ii in range(2):
        g = dot(dmu[ii * HALF : (ii + 1) * HALF, :], r1[...].reshape(ROWS, D), 1, 1) * MIX_SCALE
        g = dot(jnp.where(same_block(g.shape), g, 0.0).astype(BF16), ex_ref[...], 1, 1)
        gsec[:, 64 * ii : 64 * ii + 64] = g.astype(BF16)
    for part in range(ND):
        gss[part] = gsec[32 * part : 32 * part + 32, :]
    gs_sum.start()

    for n in range(NB):
        t = dot(act[:, blk(n, HB)], dn_ref[:, blk(n)])
        out_ref[:, blk(n)] = (mid[:, blk(n)].astype(F32) + t).astype(BF16)
    outward[0].start()
    after_y(0)
    for n in range(NB):
        h1g[:, blk(n)] = dot(dgate[:, blk(n)], gw_ref[:, blk(n)], 1, 1)
        g = dot(n1[:, blk(n)], dgate[:, blk(n)], 0, 0) * gw_ref[:, blk(n)].astype(F32)
        gcol[blk(n), :] = jnp.broadcast_to(jnp.sum(g, axis=-1, keepdims=True), (DB, 8))
    gs_sum.recv()
    gsa[me_d] = gs_sum.total().astype(BF16)
    gs_all.start()

    def block_back(ii):
        half = slice(ii * HALF, (ii + 1) * HALF)

        def unpack(rows, t):
            def store(lane, v):
                df[pl.ds(pl.multiple_of(ii * HALF + t * 32, 32), 32), lane : lane + 128] = v.astype(BF16)

            unpack_lanes(r4[ii, pl.ds(pl.multiple_of(t * 4, 4), 4)], store)

        tiles(HALF, 32, unpack)
        g = (dot(df[half, :], val[half, :], 1, 1) * MIX_SCALE).astype(BF16)
        for part in range(ND):
            gfs[ii, part] = g[32 * part : 32 * part + 32]
        gf_sum[ii].start()
        dval[half, :] = dot(fb_ref[ii], df[half, :], 0, 0).astype(BF16)

    def input_gradient(ii):
        half = slice(ii * HALF, (ii + 1) * HALF)
        for n in range(NB):
            t768[:, blk(n)] = dot(dval[half, blk(n)], vw_ref[:, blk(n)], 1, 1)

        def norm_back_first(rows, t):
            at = pl.ds(pl.multiple_of(ii * HALF + t * 32, 32), 32)
            v = x_ref[at, :].astype(F32)
            f1 = factor_of(v)
            u1 = v * f1
            s = (t768[rows, :] + h1g[at, :]) * g1
            d = dmid[at, :].astype(F32) + f1 * (s - u1 * jnp.mean(s * u1, axis=-1, keepdims=True))
            gin_ref[at, :] = d.astype(BF16)

        tiles(HALF, 32, norm_back_first)
        outward[1 + ii].start()

    def share_mixing(ii):
        gf_sum[ii].recv()
        gfa[ii, me_d] = gf_sum[ii].total().astype(BF16)
        gf_all[ii].start()

    loaded("fold", "ufold")
    for ct in range(3):
        ex4[ct].recv()
    block_back(0)
    input_gradient(0)
    after_y(1)
    share_mixing(0)
    ex4[3].recv()
    block_back(1)

    place = lax.broadcasted_iota(jnp.int32, (DB, 64), 1)
    for n in range(NB):
        g = dot(n1[:, blk(n)], dval[:, blk(n)], 0, 0)
        first = jnp.sum(g * vw_ref[:, blk(n)].astype(F32), axis=-1, keepdims=True) + gcol[blk(n), 0:1]
        columns = jnp.where(place == 0, first * inv1[blk(n), 0:1], jnp.where(place == 1, gcol2[blk(n), 0:1], 0.0))
        grad_v = dot(p3_ref[...], g.astype(BF16), 1, 1).astype(BF16)
        gains = dot(p3_ref[...], columns.astype(BF16)).astype(BF16)
        moved = jnp.concatenate([grad_v, gains], axis=1)
        cs_l[0, n] = moved[:96]
        cs_l[1, n] = moved[96:]
        to_core[2][n].start()
    for n in range(NB):
        after_core(2, n)
    dd, uu = after_x(0), after_x(1)
    folded = dot(fold_ref[:, 0:48], dd[:, 0:512]) + dot(fold_ref[:, 48:96], dd[:, 512:1024])
    fs[:, :, :] = folded.astype(BF16).reshape(16, 16, 512)
    tail = dot(fold_ref[:, 96:144], dd[:, 1024:1152]).astype(BF16).reshape(16, 16, 128)
    fs[:, :, 0:128] = fs[:, :, 0:128] + tail
    for h in range(NXH):
        u = uu[:, DB * h : DB * h + DB]
        low = dot(ufold_ref[:, 0:96], u).astype(BF16).reshape(8, 16, DB)
        high = dot(ufold_ref[:, 96:192], u).astype(BF16).reshape(8, 16, DB)
        at = slice(8 * h, 8 * h + 8)
        fs[at, :, 0:DB] = fs[at, :, 0:DB] + low
        fs[at, :, 256 : 256 + DB] = fs[at, :, 256 : 256 + DB] + high
    to_last[0].start()
    share_mixing(1)
    input_gradient(1)
    to_y[2].recv()
    ll = to_y[2].total().astype(BF16)
    folded = dot(fold_ref[:, 0:48], ll[:, 0:128]) + dot(fold_ref[:, 48:96], ll[:, 128:256])
    fsl[...] = folded.astype(BF16).reshape(16, 16, 128)
    to_last[1].start()

    to_last[0].recv()
    early_ref[...] = to_last[0].total()
    gs_all.recv()
    for part in gf_all:
        part.recv()
    for part in range(ND):
        for ii in range(2):
            mix_ref[HALF * ii + 32 * part : HALF * ii + 32 * part + 32, :] = gfa[ii, part]
        mix_ref[512 + 16 * part : 528 + 16 * part, 0:128] = gsa[part, 0:16]
        mix_ref[512 + 16 * part : 528 + 16 * part, 128:256] = gsa[part, 16:32]
    to_last[1].recv()
    late_ref[...] = to_last[1].total()

    for part in ex1 + ex2[0] + ex2[1] + ex3[0] + ex3[1] + ex4 + [gs_sum, gs_all] + gf_sum + gf_all + to_y + to_last:
        part.sent()
    for copy in to_core[0] + to_core[1] + to_core[2] + to_x:
        copy.wait_send()
    for copy in outward:
        copy.wait()


def finish_kernel(
    out_in, gin_in, mix_ref, early_ref, late_ref, pm_ref,
    out_hbm, gin_hbm, gv_ref, gg_ref, go_ref, gu_ref, gd_ref, g1_ref, g2_ref, gfirst_ref, gsecond_ref,
    spread, out_v, gin_v, sem,
):
    parts = [
        (a.at[pl.ds(128 * q, 128)], v.at[pl.ds(128 * q, 128)], b.at[pl.ds(128 * q, 128)])
        for q in range(4)
        for a, v, b in ((out_in, out_v, out_hbm), (gin_in, gin_v, gin_hbm))
    ]
    inward = [pltpu.make_async_copy(a, v, sem.at[k]) for k, (a, v, b) in enumerate(parts)]
    outward = [pltpu.make_async_copy(v, b, sem.at[8 + k]) for k, (a, v, b) in enumerate(parts)]
    for copy in inward:
        copy.start()
    for here, there in zip(inward, outward):
        here.wait()
        there.start()
    for ii in range(2):
        gfirst_ref[ii] = mix_ref[HALF * ii : HALF * ii + HALF, :].astype(F32)
    for part in range(ND):
        spread[32 * part : 32 * part + 16, :] = mix_ref[512 + 16 * part : 528 + 16 * part, 0:128]
        spread[32 * part + 16 : 32 * part + 32, :] = mix_ref[512 + 16 * part : 528 + 16 * part, 128:256]
    gsecond_ref[...] = dot(pm_ref[0:HALF, :], spread[:, 0:64], 0, 0) + dot(pm_ref[HALF:ROWS, :], spread[:, 64:128], 0, 0)
    total, late = early_ref[...] * ROW_SCALE, late_ref[...] * ROW_SCALE
    gd_ref[:, 0:512] = total[0:3]
    gd_ref[:, 512:768] = total[3:6, 0:256]
    gg_ref[...] = total[3:6, 256:448]
    go_ref[:, 0:64] = total[3:6, 448:512]
    go_ref[:, 64:192] = total[6:9, 0:128]
    gu_ref[0:6, :] = total[9:15, 0:192]
    gu_ref[6:12, :] = total[9:15, 256:448]
    gv_ref[:, 0:128] = late[0:3]
    gv_ref[:, 128:192] = late[3:6, 0:64]

    def across(column):
        square = lax.broadcasted_iota(jnp.int32, (8, 128), 0) == lax.broadcasted_iota(jnp.int32, (8, 128), 1)
        return jnp.sum(jnp.where(square, column, 0.0), axis=0, keepdims=True)[:, 0:3]

    pad = jnp.zeros((5, 1), F32)
    g2_ref[...] = across(jnp.concatenate([late[3:6, 65:66], pad], axis=0))
    g1_ref[...] = across(jnp.concatenate([late[3:6, 64:65], pad], axis=0))
    for copy in outward:
        copy.wait()


def vmem_specs(count):
    return [pl.BlockSpec(memory_space=pltpu.VMEM)] * count


def any_specs(count):
    return [pl.BlockSpec(memory_space=pl.ANY)] * count


def body(inputs, cotangent, gain_first, gain_second, value_w, gate_w, out_w, up_w, down_w, first_blocks, second_blocks):
    perm_m, expand, perm3, perm12, fold, ufold = [jnp.asarray(a, BF16) for a in constants()]
    shape = jax.ShapeDtypeStruct
    vm = lambda *s: pltpu.VMEM(s, BF16)
    vf = lambda *s: pltpu.VMEM(s, F32)
    big = lambda: vm(ROWS, D)
    dma = pltpu.SemaphoreType.DMA
    out, gin, mix, early, late = pl.pallas_call(
        main_kernel,
        out_shape=[
            shape((ROWS, D), BF16), shape((ROWS, D), BF16), shape((640, 256), BF16), shape((16, 512), F32),
            shape((16, 128), F32),
        ],
        in_specs=any_specs(2) + vmem_specs(2) + any_specs(13),
        out_specs=any_specs(2) + vmem_specs(3),
        scratch_shapes=[
            big(), big(), vm(DB, D), vm(DB, D), vm(DB, D), vm(DB, NB * HB), vm(D, D), vm(2, 256, 256), vm(512, 64),
            vm(512, 512), vm(64, 512), vm(192, 192), vm(192, 192), vm(256, 144), vm(128, 192), big(), big(),
            big(), big(), big(), big(), big(), big(), big(), big(), big(), big(), big(),
            vm(ROWS, NB * HB), vm(ROWS, NB * HB), vf(2, NB, HALF, HB),
            vm(2, HALF, ROWS), big(), vf(HALF, D), vf(HALF, HB), vf(ROWS, D),
            vm(NS, 16, D), vm(NS, 16, D), vm(2, NS, 16, 384), vm(2, NS, 16, 384),
            vm(2, NS, 16, 384), vm(2, NS, 16, 384), vm(2, NS, 16, 384), vm(2, NS, 16, 384),
            vm(ND, 32, 128), vm(ND, 32, 128), vm(ND, 32, 128), vm(2, ND, 32, 256), vm(2, ND, 32, 256), vm(2, ND, 32, 256),
            vm(HALF, 128), vf(D, 8), vf(D, 8), vm(DB, DL),
            vm(2, NB, 96, DL), vm(2, NB, 96, UL), vm(2, NB, 96, LW), vm(NB, 96, DL), vm(NB, 96, UL), vm(NB, 96, LW),
            vm(NY, 96, DL), vm(NY, 96, UL), vm(ND, 48, LW), vm(NY, 96, DL), vm(NY, 96, UL), vm(ND, 48, LW),
            vm(2, 48, DL), vm(2, 96, 384), vm(48, DL), vm(96, 384),
            vm(16, 16, 512), vm(16, 16, 512), vm(16, 16, 128), vm(16, 16, 128),
            dma((SEMS,)), dma((SEMS,)), dma((18,)),
        ],
        compiler_params=pltpu.CompilerParams(
            collective_id=0, has_side_effects=True, vmem_limit_bytes=VMEM_LIMIT
        ),
    )(
        inputs.reshape(ROWS, D), cotangent.reshape(ROWS, D), gain_first, gain_second,
        value_w, gate_w, out_w, up_w, down_w, first_blocks, second_blocks.reshape(512, 64),
        perm_m, expand, perm3, perm12, fold, ufold,
    )
    out, gin, gv, gg, go, gu, gd, g1, g2, gfirst, gsecond = pl.pallas_call(
        finish_kernel,
        out_shape=[
            shape((ROWS, D), BF16), shape((ROWS, D), BF16), shape((3, DB), F32), shape((3, DB), F32), shape((3, DB), F32),
            shape((12, DB), F32), shape((3, HB), F32), shape((1, 3), F32), shape((1, 3), F32), shape((2, 256, 256), F32),
            shape((512, 64), F32),
        ],
        in_specs=any_specs(2) + vmem_specs(4),
        out_specs=any_specs(2) + vmem_specs(9),
        scratch_shapes=[vm(HALF, 128), big(), big(), dma((16,))],
    )(out, gin, mix, early, late, perm_m)
    return (
        out.reshape(1, ROWS, D), gin.reshape(1, ROWS, D), gv.T, gg.T, go.T, gu.T, gd.T, g1.reshape(3), g2.reshape(3),
        gfirst, gsecond.reshape(8, 64, 64),
    )


def solution(mesh):
    tokens, whole = P("dp", "seq", None), P("seq", None, None)
    columns = P(None, ("dp", "seq"))
    gains = P(("dp", "seq"))
    return jax.shard_map(
        body,
        mesh=mesh,
        in_specs=(tokens, tokens, P(), P(), P(), P(), P(), P(), P(), whole, whole),
        out_specs=(tokens, tokens, columns, columns, columns, columns, columns, gains, gains, whole, whole),
        check_vma=False,
    )
```

```python
import functools
import math

import jax
import jax.numpy as jnp
import numpy as np
from jax import lax
from jax.experimental import pallas as pl
from jax.experimental.pallas import tpu as pltpu
from jax.sharding import PartitionSpec as P

MESH = pl.DeviceIdType.MESH
F32 = jnp.float32
BF16 = jnp.bfloat16
EPS = 1e-6
NY, NXL, NXH, NZ, NC = 4, 2, 2, 8, 2
NS, ND = NXH * NZ * NC, NY * NXL
D, NB, DB, HB, ROWS, HALF = 768, 4, 192, 768, 512, 256
ROW_SCALE = 1.0 / math.sqrt(131072.0)
MIX_SCALE = 1.0 / math.sqrt(6144.0)
DL, UL, LW = 1152, 768, 256
A1, A2, A2B, A3, A3B, A4, GS, GF, CORE, YY, XX, LAST = 0, 3, 6, 7, 8, 11, 15, 17, 21, 33, 36, 38
SEMS = 40
VMEM_LIMIT = 60 * 2**20


def dot(a, b, ca=1, cb=0):
    return lax.dot_general(a, b, (((ca,), (cb,)), ((), ())), preferred_element_type=F32)


def constants():
    one = lambda shape, pairs: _onehot(shape, pairs)
    row, col = [], []
    for ii in range(2):
        for d in range(NS):
            for bl in range(8):
                row.append(ii * 256 + d * 8 + bl)
                col.append(bl * 64 + 2 * d + ii)
    perm_m = one((512, 512), (row, col))
    expand = one((64, 512), (np.arange(512) // 8, np.arange(512)))
    out = np.arange(192)
    c, rem = out // 96, out % 96
    perm3 = one((192, 192), (out, rem // 3 * 6 + c * 3 + rem % 3))
    perm12 = one((192, 192), (out, rem // 12 * 24 + c * 12 + rem % 12))
    dest, t = np.arange(48) // 3, np.arange(48) % 3
    fold = np.concatenate([one((256, 48), (dest * 16 + 3 * f + t, np.arange(48))) for f in range(3)], axis=1)
    z, t = np.arange(96) // 12, np.arange(96) % 12
    low, high = t < 6, t >= 6
    ufold = np.concatenate(
        [
            one((128, 96), ((z * 16 + 9 + t)[low], np.arange(96)[low])),
            one((128, 96), ((z * 16 + 3 + t)[high], np.arange(96)[high])),
        ],
        axis=1,
    )
    return perm_m, expand, perm3, perm12, fold, ufold


def _onehot(shape, pairs):
    array = np.zeros(shape, np.float32)
    array[pairs[0], pairs[1]] = 1.0
    return array


def remote(src, dst, ssem, rsem, device):
    return pltpu.make_async_remote_copy(
        src_ref=src, dst_ref=dst, send_sem=ssem, recv_sem=rsem, device_id=device, device_id_type=MESH
    )


def each_seq_peer(me, act):
    xh, z, c = me // 16, lax.rem(me // 2, 8), lax.rem(me, 2)
    corners = [(1 - xh) * 16 + c, (1 - xh) * 16 + 1 - c, xh * 16 + 1 - c, xh * 16 + c]

    def step(t, carry):
        dz = 4 + (1 - 2 * lax.rem(t, 2)) * ((t + 1) // 2)
        there = lax.rem(z + dz, 8) * 2
        for corner in corners:
            act(corner + there)
        return carry

    lax.fori_loop(0, 7, step, 0)
    for corner in corners[:3]:
        act(corner + z * 2)


def greet(me_s, me_d):
    barrier = pltpu.get_barrier_semaphore()

    def over_seq(peer):
        pl.semaphore_signal(barrier, inc=1, device_id={"seq": peer}, device_id_type=MESH)

    def over_dp(k, carry):
        pl.semaphore_signal(barrier, inc=1, device_id={"dp": lax.rem(me_d + k, ND)}, device_id_type=MESH)
        return carry

    each_seq_peer(me_s, over_seq)
    lax.fori_loop(1, ND, over_dp, 0)
    return lambda: pl.semaphore_wait(barrier, NS - 1 + ND - 1)


class Exchange:
    def __init__(self, sbuf, rbuf, ssem, rsem, me, lanes=None):
        self.me, self.sems = me, (ssem, rsem)
        self.sbuf, self.rbuf, self.lanes = sbuf, rbuf, lanes

    def at(self, ref, index):
        return ref.at[index] if self.lanes is None else ref.at[index, :, self.lanes]

    def start(self):
        def send(peer):
            remote(self.at(self.sbuf, peer), self.at(self.rbuf, self.me), *self.sems, {"seq": peer}).start()

        each_seq_peer(self.me, send)
        if self.lanes is None:
            self.rbuf[self.me] = self.sbuf[self.me]
        else:
            self.rbuf[self.me, :, self.lanes] = self.sbuf[self.me, :, self.lanes]

    def whole(self):
        part = pl.ds(0, NS - 1)
        return remote(self.at(self.sbuf, part), self.at(self.rbuf, part), *self.sems, {"seq": self.me})

    def recv(self):
        self.whole().wait_recv()

    def sent(self):
        self.whole().wait_send()


class Ring:
    def __init__(self, sbuf, rbuf, ssem, rsem, me, count, device, same=False):
        self.sbuf, self.rbuf, self.sems = sbuf, rbuf, (ssem, rsem)
        self.me, self.count, self.device, self.same = me, count, device, same

    def one(self, to):
        remote(self.sbuf.at[to], self.rbuf.at[self.me], *self.sems, self.device(to)).start()

    def own(self, to):
        self.rbuf[to] = self.sbuf[to]

    def start(self):
        def send(k, carry):
            to = lax.rem(self.me + k, self.count)
            source = self.sbuf.at[self.me if self.same else to]
            remote(source, self.rbuf.at[self.me], *self.sems, self.device(to)).start()
            return carry

        lax.fori_loop(1, self.count, send, 0)
        if not self.same:
            self.rbuf[self.me] = self.sbuf[self.me]

    def whole(self):
        part = pl.ds(0, self.count - 1)
        return remote(self.sbuf.at[part], self.rbuf.at[part], *self.sems, self.device(self.me))

    def recv(self):
        self.whole().wait_recv()

    def sent(self):
        self.whole().wait_send()

    def total(self):
        out = self.rbuf[0].astype(F32)
        for k in range(1, self.count):
            out = out + self.rbuf[k].astype(F32)
        return out


def tiles(rows, tile, body):
    def step(t, carry):
        body(pl.ds(pl.multiple_of(t * tile, tile), tile), t)
        return carry

    lax.fori_loop(0, rows // tile, step, 0)


def blk(n, width=DB):
    return slice(n * width, (n + 1) * width)


def unpack_lanes(packed, store):
    count = packed.shape[0]
    for t in range(3):
        v = packed[:, :, 128 * t : 128 * t + 128].astype(F32).reshape(count, 2, 8, 128)
        store(256 * t, v[:, 0].reshape(count * 8, 128))
        store(256 * t + 128, v[:, 1].reshape(count * 8, 128))


def pack_pair(low, high):
    count = low.shape[0] // 8
    both = jnp.concatenate([low.reshape(count, 8, -1), high.reshape(count, 8, -1)], axis=1)
    return both.astype(BF16)


def factor_of(rows):
    return lax.rsqrt(jnp.mean(rows * rows, axis=-1, keepdims=True) + EPS)


def gelu_pair(h):
    size = jnp.abs(h)
    den = 1.0 + (0.3275911 / math.sqrt(2.0)) * size
    t = pl.reciprocal(den, approx=True)
    t = t * (2.0 - den * t)
    e = jnp.exp(-0.5 * (h * h))
    poly = 0.5 * 1.061405429
    for a in (-1.453152027, 1.421413741, -0.284496736, 0.254829592):
        poly = poly * t + 0.5 * a
    q = poly * t * e
    cdf = jnp.where(h >= 0.0, 1.0 - q, q)
    return h * cdf, cdf + h * (e * (1.0 / math.sqrt(2.0 * math.pi)))


def same_block(shape):
    return (lax.broadcasted_iota(jnp.int32, shape, 0) & 7) == (lax.broadcasted_iota(jnp.int32, shape, 1) & 7)


def main_kernel(
    x_hbm, cot_hbm, g1_ref, g2_ref, vw_hbm, gw_hbm, ow_hbm, up_hbm, dn_hbm, fb_hbm, sb_hbm,
    pm_hbm, ex_hbm, p3_hbm, p12_hbm, fold_hbm, ufold_hbm,
    out_hbm, gin_hbm, mix_ref, early_ref, late_ref,
    x_ref, cot_ref, vw_ref, gw_ref, ow_ref, up_ref, dn_ref, fb_ref, sb_ref,
    pm_ref, ex_ref, p3_ref, p12_ref, fold_ref, ufold_ref, out_ref, gin_ref,
    n1, val, gate, mixed, y, mid, n2, dmid, dgate, df, dval, act, dpre, dact, mm, dmu, t768, hbuf, h1g,
    s1, r1, s2, r2, s3, r3, s4, r4, gss, gsr, gsa, gfs, gfr, gfa, gsec, gcol, gcol2, tmp,
    cs_d, cs_u, cs_l, cr_d, cr_u, cr_l, ys_d, ys_u, ys_l, yr_d, yr_u, yr_l,
    xs_d, xs_u, xr_d, xr_u, fs, fr, fsl, frl,
    ssem, rsem, lsem,
):
    me_s, me_d = lax.axis_index("seq"), lax.axis_index("dp")
    yy, xl = me_d // NXL, lax.rem(me_d, NXL)
    hz, core = me_s // NC, lax.rem(me_s, NC)
    all_here = greet(me_s, me_d)

    def exchange(sbuf, rbuf, index, lanes=None):
        return Exchange(sbuf, rbuf, ssem.at[index], rsem.at[index], me_s, lanes)

    def lanes_of(ct, width=256):
        return slice(width * ct, width * ct + width)

    ex1 = [exchange(s1, r1, A1 + ct, lanes_of(ct)) for ct in range(3)]
    ex2 = [
        [exchange(s2.at[0], r2.at[0], A2 + ct, lanes_of(ct, 128)) for ct in range(3)],
        [exchange(s2.at[1], r2.at[1], A2B)],
    ]
    ex3 = [
        [exchange(s3.at[0], r3.at[0], A3)],
        [exchange(s3.at[1], r3.at[1], A3B + ct, lanes_of(ct, 128)) for ct in range(3)],
    ]
    ex4 = [exchange(s4.at[0], r4.at[0], A4 + ct, lanes_of(ct, 128)) for ct in range(3)] + [exchange(s4.at[1], r4.at[1], A4 + 3)]

    def over_dp(sbuf, rbuf, index, same=False):
        return Ring(sbuf, rbuf, ssem.at[index], rsem.at[index], me_d, ND, lambda to: {"dp": to}, same)

    gs_sum, gs_all = over_dp(gss, gsr, GS), over_dp(gsa, gsa, GS + 1, True)
    gf_sum = [over_dp(gfs.at[ii], gfr.at[ii], GF + ii) for ii in range(2)]
    gf_all = [over_dp(gfa.at[ii], gfa.at[ii], GF + 2 + ii, True) for ii in range(2)]
    pieces = ((cs_d, cr_d, ys_d, yr_d, xs_d, xr_d), (cs_u, cr_u, ys_u, yr_u, xs_u, xr_u), (cs_l, cr_l, ys_l, yr_l))
    mate, beside = {"seq": hz * NC + 1 - core}, {"dp": yy * NXL + 1 - xl}
    to_core = [
        [
            remote(p[0].at[1 - core, n], p[1].at[n], ssem.at[CORE + 4 * i + n], rsem.at[CORE + 4 * i + n], mate)
            for n in range(NY)
        ]
        for i, p in enumerate(pieces)
    ]
    to_y = [
        Ring(p[2], p[3], ssem.at[YY + i], rsem.at[YY + i], yy, NY, lambda to: {"dp": to * NXL + xl})
        for i, p in enumerate(pieces[:2])
    ] + [over_dp(ys_l, yr_l, YY + 2)]
    to_x = [remote(p[4].at[1 - xl], p[5], ssem.at[XX + i], rsem.at[XX + i], beside) for i, p in enumerate(pieces[:2])]
    to_last = [
        Ring(a, b, ssem.at[LAST + i], rsem.at[LAST + i], hz, NXH * NZ, lambda to: {"seq": to * NC + core})
        for i, (a, b) in enumerate(((fs, fr), (fsl, frl)))
    ]

    def after_core(i, n):
        sent, got, ys = pieces[i][:3]
        to_core[i][n].wait_recv()
        both = (sent[core, n].astype(F32) + got[n].astype(F32)).astype(BF16)
        if i == 2:
            for h in range(NXL):
                ys[NXL * n + h] = both[48 * h : 48 * h + 48]
            if n == NY - 1:
                to_y[2].start()
        else:
            ys[n] = both

            @pl.when(yy != n)
            def _():
                to_y[i].one(n)

            @pl.when(yy == n)
            def _():
                to_y[i].own(n)

    def after_y(i):
        xs = pieces[i][4]
        to_y[i].recv()
        total = to_y[i].total()
        for h in range(NXL):
            xs[h] = (total[:, 384 * h : 384 * h + 384] if i == 1 else total[48 * h : 48 * h + 48]).astype(BF16)
        to_x[i].start()

    def after_x(i):
        xs, xr = pieces[i][4:]
        to_x[i].wait_recv()
        return (xs[xl].astype(F32) + xr[...].astype(F32)).astype(BF16)

    inward = {}
    for index, (name, source, target) in enumerate((
        ("x", x_hbm, x_ref), ("vw", vw_hbm, vw_ref), ("fb", fb_hbm, fb_ref), ("gw", gw_hbm, gw_ref), ("sb", sb_hbm, sb_ref),
        ("pm", pm_hbm, pm_ref), ("ex", ex_hbm, ex_ref), ("cot", cot_hbm, cot_ref), ("dn", dn_hbm, dn_ref),
        ("ow", ow_hbm, ow_ref), ("up", up_hbm, up_ref), ("p3", p3_hbm, p3_ref), ("p12", p12_hbm, p12_ref),
        ("fold", fold_hbm, fold_ref), ("ufold", ufold_hbm, ufold_ref),
    )):
        inward[name] = pltpu.make_async_copy(source, target, lsem.at[index])
        inward[name].start()
    outward = [pltpu.make_async_copy(out_ref, out_hbm, lsem.at[15])] + [
        pltpu.make_async_copy(
            gin_ref.at[pl.ds(HALF * ii, HALF)], gin_hbm.at[pl.ds(HALF * ii, HALF)], lsem.at[16 + ii]
        )
        for ii in range(2)
    ]

    def loaded(*names):
        for name in names:
            inward[name].wait()

    g1, g2 = g1_ref[...].reshape(1, D), g2_ref[...].reshape(1, D)

    def norm_first(rows, t):
        v = x_ref[rows, :].astype(F32)
        n1[rows, :] = (v * factor_of(v) * g1).astype(BF16)

    loaded("x")
    tiles(ROWS, 32, norm_first)
    loaded("vw", "fb")
    for ct in range(3):
        for n in ((0, 1), (2,), (3,))[ct]:
            val[:, blk(n)] = dot(n1[:, blk(n)], vw_ref[:, blk(n)]).astype(BF16)
        lanes = lanes_of(ct)
        pair = [dot(fb_ref[ii], val[ii * HALF : (ii + 1) * HALF, lanes]) for ii in range(2)]
        s1[:, :, lanes] = pack_pair(*pair)
        if ct == 0:
            all_here()
        ex1[ct].start()

    loaded("sb", "pm", "ex")
    spread = dot(pm_ref[...], sb_ref[...]).astype(BF16)
    for ii in range(2):
        wide = dot(spread[ii * HALF : (ii + 1) * HALF], ex_ref[...])
        mm[ii] = jnp.where(same_block(wide.shape), wide, 0.0).astype(BF16)
    loaded("gw")
    for n in range(NB):
        gate[:, blk(n)] = dot(n1[:, blk(n)], gw_ref[:, blk(n)]).astype(BF16)
    loaded("cot", "dn")
    for n in range(NB):
        for ii in range(2):
            dact[ii, n] = dot(cot_ref[ii * HALF : (ii + 1) * HALF, blk(n)], dn_ref[:, blk(n)], 1, 1)

    for ct in range(3):
        ex1[ct].recv()
        lanes = lanes_of(ct)
        for ii in range(2):
            o = dot(mm[ii], r1[:, :, lanes].reshape(NS * 16, 256))
            s2[ii, :, :, 128 * ct : 128 * ct + 128] = pack_pair(o[:, :128], o[:, 128:])
            if ii == 0:
                ex2[0][ct].start()
    ex2[1][0].start()
    loaded("ow", "up")

    def token_half(ii):
        base = ii * HALF
        half = slice(base, base + HALF)

        def rows_of(rows):
            return pl.ds(pl.multiple_of(base + rows.start, rows.size), rows.size)

        for part in ex2[ii]:
            part.recv()

        def gated(rows, t):
            part = r2[ii, pl.ds(pl.multiple_of(t * 4, 4), 4)]

            def store(lane, v):
                at = (rows_of(rows), slice(lane, lane + 128))
                mixed[at] = v.astype(BF16)
                y[at] = (v * gate[at].astype(F32)).astype(BF16)

            unpack_lanes(part, store)

        tiles(HALF, 32, gated)
        for n in range(NB):
            t768[:, blk(n)] = dot(y[half, blk(n)], ow_ref[:, blk(n)])

        def norm_second(rows, t):
            m = (x_ref[rows_of(rows), :].astype(F32) + t768[rows, :]).astype(BF16)
            mid[rows_of(rows), :] = m
            mf = m.astype(F32)
            n2[rows_of(rows), :] = (mf * factor_of(mf) * g2).astype(BF16)

        tiles(HALF, 64, norm_second)
        for n in range(NB):
            hbuf[...] = dot(n2[half, blk(n)], up_ref[:, blk(n, HB)])

            def gelu(rows, t):
                for lt in range(3):
                    lanes = slice(256 * lt, 256 * lt + 256)
                    wide = slice(n * HB + 256 * lt, n * HB + 256 * lt + 256)
                    value, slope = gelu_pair(hbuf[rows, lanes])
                    act[rows_of(rows), wide] = value.astype(BF16)
                    dpre[rows_of(rows), wide] = (slope * dact[ii, n, rows, lanes]).astype(BF16)

            tiles(HALF, 64, gelu)
            t768[:, blk(n)] = dot(dpre[half, blk(n, HB)], up_ref[:, blk(n, HB)], 1, 1)

        def norm_back_second(rows, t):
            mf = mid[rows_of(rows), :].astype(F32)
            f2 = factor_of(mf)
            u2 = mf * f2
            h2 = t768[rows, :]
            s = h2 * g2
            d = cot_ref[rows_of(rows), :].astype(F32) + f2 * (s - u2 * jnp.mean(s * u2, axis=-1, keepdims=True))
            dmid[rows_of(rows), :] = d.astype(BF16)

        tiles(HALF, 64, norm_back_second)
        for n in range(NB):
            t768[:, blk(n)] = dot(dmid[half, blk(n)], ow_ref[:, blk(n)], 1, 1)

        def gates_back(rows, t):
            dy = t768[rows, :]
            at = rows_of(rows)
            dgate[at, :] = (dy * mixed[at, :].astype(F32)).astype(BF16)
            dm = dy * gate[at, :].astype(F32)
            for ct in range(3):
                low, high = dm[:, 256 * ct : 256 * ct + 128], dm[:, 256 * ct + 128 : 256 * ct + 256]
                s3[ii, pl.ds(pl.multiple_of(t * 4, 4), 4), :, 128 * ct : 128 * ct + 128] = pack_pair(low, high)

        tiles(HALF, 32, gates_back)
        for part in ex3[ii]:
            part.start()

    token_half(0)
    token_half(1)

    def unpack_mixed(ii, ct):
        def step(rows, t):
            v = r3[ii, pl.ds(pl.multiple_of(t * 4, 4), 4), :, 128 * ct : 128 * ct + 128].astype(F32).reshape(4, 2, 8, 128)
            at = pl.ds(pl.multiple_of(ii * HALF + t * 32, 32), 32)
            for h in range(2):
                lane = 256 * ct + 128 * h
                dmu[at, lane : lane + 128] = v[:, h].reshape(32, 128).astype(BF16)

        tiles(HALF, 32, step)

    def second_back(ct):
        if ct == 0:
            ex3[0][0].recv()
            for every in range(3):
                unpack_mixed(0, every)
        ex3[1][ct].recv()
        unpack_mixed(1, ct)
        lanes = lanes_of(ct)
        o = dot(mm[...].reshape(ROWS, ROWS), dmu[:, lanes], 0, 0).reshape(NS, 2, 8, 256)
        for ii in range(2):
            low, high = o[:, ii, :, :128].reshape(HALF, 128), o[:, ii, :, 128:].reshape(HALF, 128)
            s4[ii, :, :, 128 * ct : 128 * ct + 128] = pack_pair(low, high)
        ex4[ct].start()
        if ct == 2:
            ex4[3].start()

    loaded("p3", "p12")
    inv1 = jnp.broadcast_to(1.0 / g1, (8, D)).T
    inv2 = jnp.broadcast_to(1.0 / g2, (8, D)).T

    def piece_down(n):
        tmp[:, 0:D] = dot(cot_ref[:, blk(n)], act[:, blk(n, HB)], 0, 0).astype(BF16)
        tmp[:, D : D + DB] = dot(dgate[:, blk(n)], n1[:, blk(n)], 0, 0).astype(BF16)
        tmp[:, D + DB : DL] = dot(dmid[:, blk(n)], y[:, blk(n)], 0, 0).astype(BF16)
        moved = dot(p3_ref[...], tmp[...]).astype(BF16)
        cs_d[0, n] = moved[:96]
        cs_d[1, n] = moved[96:]
        to_core[0][n].start()

    def piece_up(n):
        g = dot(n2[:, blk(n)], dpre[:, blk(n, HB)], 0, 0)
        column = jnp.sum(g * up_ref[:, blk(n, HB)].astype(F32), axis=-1, keepdims=True) * inv2[blk(n), 0:1]
        gcol2[blk(n), :] = jnp.broadcast_to(column, (DB, 8))
        for q in range(4):
            moved = dot(p12_ref[...], g[:, blk(q)].astype(BF16), 1, 1).astype(BF16)
            cs_u[0, n, :, blk(q)] = moved[:96]
            cs_u[1, n, :, blk(q)] = moved[96:]
        to_core[1][n].start()

    piece_down(0)
    piece_down(1)
    after_core(0, 0)
    piece_down(2)
    after_core(0, 1)
    piece_down(3)
    after_core(0, 2)
    second_back(0)
    piece_up(0)
    after_core(0, 3)
    piece_up(1)
    after_core(1, 0)
    second_back(1)
    piece_up(2)
    after_core(1, 1)
    piece_up(3)
    after_core(1, 2)
    second_back(2)
    after_core(1, 3)

    for ii in range(2):
        g = dot(dmu[ii * HALF : (ii + 1) * HALF, :], r1[...].reshape(ROWS, D), 1, 1) * MIX_SCALE
        g = dot(jnp.where(same_block(g.shape), g, 0.0).astype(BF16), ex_ref[...], 1, 1)
        gsec[:, 64 * ii : 64 * ii + 64] = g.astype(BF16)
    for part in range(ND):
        gss[part] = gsec[32 * part : 32 * part + 32, :]
    gs_sum.start()

    for n in range(NB):
        t = dot(act[:, blk(n, HB)], dn_ref[:, blk(n)])
        out_ref[:, blk(n)] = (mid[:, blk(n)].astype(F32) + t).astype(BF16)
    outward[0].start()
    after_y(0)
    for n in range(NB):
        h1g[:, blk(n)] = dot(dgate[:, blk(n)], gw_ref[:, blk(n)], 1, 1)
        g = dot(n1[:, blk(n)], dgate[:, blk(n)], 0, 0) * gw_ref[:, blk(n)].astype(F32)
        gcol[blk(n), :] = jnp.broadcast_to(jnp.sum(g, axis=-1, keepdims=True), (DB, 8))
    gs_sum.recv()
    gsa[me_d] = gs_sum.total().astype(BF16)
    gs_all.start()

    def block_back(ii):
        half = slice(ii * HALF, (ii + 1) * HALF)

        def unpack(rows, t):
            def store(lane, v):
                df[pl.ds(pl.multiple_of(ii * HALF + t * 32, 32), 32), lane : lane + 128] = v.astype(BF16)

            unpack_lanes(r4[ii, pl.ds(pl.multiple_of(t * 4, 4), 4)], store)

        tiles(HALF, 32, unpack)
        g = (dot(df[half, :], val[half, :], 1, 1) * MIX_SCALE).astype(BF16)
        for part in range(ND):
            gfs[ii, part] = g[32 * part : 32 * part + 32]
        gf_sum[ii].start()
        dval[half, :] = dot(fb_ref[ii], df[half, :], 0, 0).astype(BF16)

    def input_gradient(ii):
        half = slice(ii * HALF, (ii + 1) * HALF)
        for n in range(NB):
            t768[:, blk(n)] = dot(dval[half, blk(n)], vw_ref[:, blk(n)], 1, 1)

        def norm_back_first(rows, t):
            at = pl.ds(pl.multiple_of(ii * HALF + t * 32, 32), 32)
            v = x_ref[at, :].astype(F32)
            f1 = factor_of(v)
            u1 = v * f1
            s = (t768[rows, :] + h1g[at, :]) * g1
            d = dmid[at, :].astype(F32) + f1 * (s - u1 * jnp.mean(s * u1, axis=-1, keepdims=True))
            gin_ref[at, :] = d.astype(BF16)

        tiles(HALF, 32, norm_back_first)
        outward[1 + ii].start()

    def share_mixing(ii):
        gf_sum[ii].recv()
        gfa[ii, me_d] = gf_sum[ii].total().astype(BF16)
        gf_all[ii].start()

    loaded("fold", "ufold")
    for ct in range(3):
        ex4[ct].recv()
    block_back(0)
    input_gradient(0)
    after_y(1)
    share_mixing(0)
    ex4[3].recv()
    block_back(1)

    place = lax.broadcasted_iota(jnp.int32, (DB, 64), 1)
    for n in range(NB):
        g = dot(n1[:, blk(n)], dval[:, blk(n)], 0, 0)
        first = jnp.sum(g * vw_ref[:, blk(n)].astype(F32), axis=-1, keepdims=True) + gcol[blk(n), 0:1]
        columns = jnp.where(place == 0, first * inv1[blk(n), 0:1], jnp.where(place == 1, gcol2[blk(n), 0:1], 0.0))
        grad_v = dot(p3_ref[...], g.astype(BF16), 1, 1).astype(BF16)
        gains = dot(p3_ref[...], columns.astype(BF16)).astype(BF16)
        moved = jnp.concatenate([grad_v, gains], axis=1)
        cs_l[0, n] = moved[:96]
        cs_l[1, n] = moved[96:]
        to_core[2][n].start()
    for n in range(NB):
        after_core(2, n)
    dd, uu = after_x(0), after_x(1)
    folded = dot(fold_ref[:, 0:48], dd[:, 0:512]) + dot(fold_ref[:, 48:96], dd[:, 512:1024])
    fs[:, :, :] = folded.astype(BF16).reshape(16, 16, 512)
    tail = dot(fold_ref[:, 96:144], dd[:, 1024:1152]).astype(BF16).reshape(16, 16, 128)
    fs[:, :, 0:128] = fs[:, :, 0:128] + tail
    for h in range(NXH):
        u = uu[:, DB * h : DB * h + DB]
        low = dot(ufold_ref[:, 0:96], u).astype(BF16).reshape(8, 16, DB)
        high = dot(ufold_ref[:, 96:192], u).astype(BF16).reshape(8, 16, DB)
        at = slice(8 * h, 8 * h + 8)
        fs[at, :, 0:DB] = fs[at, :, 0:DB] + low
        fs[at, :, 256 : 256 + DB] = fs[at, :, 256 : 256 + DB] + high
    to_last[0].start()
    share_mixing(1)
    input_gradient(1)
    to_y[2].recv()
    ll = to_y[2].total().astype(BF16)
    folded = dot(fold_ref[:, 0:48], ll[:, 0:128]) + dot(fold_ref[:, 48:96], ll[:, 128:256])
    fsl[...] = folded.astype(BF16).reshape(16, 16, 128)
    to_last[1].start()

    to_last[0].recv()
    early_ref[...] = to_last[0].total()
    gs_all.recv()
    for part in gf_all:
        part.recv()
    for part in range(ND):
        for ii in range(2):
            mix_ref[HALF * ii + 32 * part : HALF * ii + 32 * part + 32, :] = gfa[ii, part]
        mix_ref[512 + 16 * part : 528 + 16 * part, 0:128] = gsa[part, 0:16]
        mix_ref[512 + 16 * part : 528 + 16 * part, 128:256] = gsa[part, 16:32]
    to_last[1].recv()
    late_ref[...] = to_last[1].total()

    for part in ex1 + ex2[0] + ex2[1] + ex3[0] + ex3[1] + ex4 + [gs_sum, gs_all] + gf_sum + gf_all + to_y + to_last:
        part.sent()
    for copy in to_core[0] + to_core[1] + to_core[2] + to_x:
        copy.wait_send()
    for copy in outward:
        copy.wait()


def finish_kernel(
    out_in, gin_in, mix_ref, early_ref, late_ref, pm_ref,
    out_hbm, gin_hbm, gv_ref, gg_ref, go_ref, gu_ref, gd_ref, g1_ref, g2_ref, gfirst_ref, gsecond_ref,
    spread, out_v, gin_v, sem,
):
    parts = [
        (a.at[pl.ds(128 * q, 128)], v.at[pl.ds(128 * q, 128)], b.at[pl.ds(128 * q, 128)])
        for q in range(4)
        for a, v, b in ((out_in, out_v, out_hbm), (gin_in, gin_v, gin_hbm))
    ]
    inward = [pltpu.make_async_copy(a, v, sem.at[k]) for k, (a, v, b) in enumerate(parts)]
    outward = [pltpu.make_async_copy(v, b, sem.at[8 + k]) for k, (a, v, b) in enumerate(parts)]
    for copy in inward:
        copy.start()
    for here, there in zip(inward, outward):
        here.wait()
        there.start()
    for ii in range(2):
        gfirst_ref[ii] = mix_ref[HALF * ii : HALF * ii + HALF, :].astype(F32)
    for part in range(ND):
        spread[32 * part : 32 * part + 16, :] = mix_ref[512 + 16 * part : 528 + 16 * part, 0:128]
        spread[32 * part + 16 : 32 * part + 32, :] = mix_ref[512 + 16 * part : 528 + 16 * part, 128:256]
    gsecond_ref[...] = dot(pm_ref[0:HALF, :], spread[:, 0:64], 0, 0) + dot(pm_ref[HALF:ROWS, :], spread[:, 64:128], 0, 0)
    total, late = early_ref[...] * ROW_SCALE, late_ref[...] * ROW_SCALE
    gd_ref[:, 0:512] = total[0:3]
    gd_ref[:, 512:768] = total[3:6, 0:256]
    gg_ref[...] = total[3:6, 256:448]
    go_ref[:, 0:64] = total[3:6, 448:512]
    go_ref[:, 64:192] = total[6:9, 0:128]
    gu_ref[0:6, :] = total[9:15, 0:192]
    gu_ref[6:12, :] = total[9:15, 256:448]
    gv_ref[:, 0:128] = late[0:3]
    gv_ref[:, 128:192] = late[3:6, 0:64]

    def across(column):
        square = lax.broadcasted_iota(jnp.int32, (8, 128), 0) == lax.broadcasted_iota(jnp.int32, (8, 128), 1)
        return jnp.sum(jnp.where(square, column, 0.0), axis=0, keepdims=True)[:, 0:3]

    pad = jnp.zeros((5, 1), F32)
    g2_ref[...] = across(jnp.concatenate([late[3:6, 65:66], pad], axis=0))
    g1_ref[...] = across(jnp.concatenate([late[3:6, 64:65], pad], axis=0))
    for copy in outward:
        copy.wait()


def vmem_specs(count):
    return [pl.BlockSpec(memory_space=pltpu.VMEM)] * count


def any_specs(count):
    return [pl.BlockSpec(memory_space=pl.ANY)] * count


def body(inputs, cotangent, gain_first, gain_second, value_w, gate_w, out_w, up_w, down_w, first_blocks, second_blocks):
    perm_m, expand, perm3, perm12, fold, ufold = [jnp.asarray(a, BF16) for a in constants()]
    shape = jax.ShapeDtypeStruct
    vm = lambda *s: pltpu.VMEM(s, BF16)
    vf = lambda *s: pltpu.VMEM(s, F32)
    big = lambda: vm(ROWS, D)
    dma = pltpu.SemaphoreType.DMA
    out, gin, mix, early, late = pl.pallas_call(
        main_kernel,
        out_shape=[
            shape((ROWS, D), BF16), shape((ROWS, D), BF16), shape((640, 256), BF16), shape((16, 512), F32),
            shape((16, 128), F32),
        ],
        in_specs=any_specs(2) + vmem_specs(2) + any_specs(13),
        out_specs=any_specs(2) + vmem_specs(3),
        scratch_shapes=[
            big(), big(), vm(DB, D), vm(DB, D), vm(DB, D), vm(DB, NB * HB), vm(D, D), vm(2, 256, 256), vm(512, 64),
            vm(512, 512), vm(64, 512), vm(192, 192), vm(192, 192), vm(256, 144), vm(128, 192), big(), big(),
            big(), big(), big(), big(), big(), big(), big(), big(), big(), big(), big(),
            vm(ROWS, NB * HB), vm(ROWS, NB * HB), vf(2, NB, HALF, HB),
            vm(2, HALF, ROWS), big(), vf(HALF, D), vf(HALF, HB), vf(ROWS, D),
            vm(NS, 16, D), vm(NS, 16, D), vm(2, NS, 16, 384), vm(2, NS, 16, 384),
            vm(2, NS, 16, 384), vm(2, NS, 16, 384), vm(2, NS, 16, 384), vm(2, NS, 16, 384),
            vm(ND, 32, 128), vm(ND, 32, 128), vm(ND, 32, 128), vm(2, ND, 32, 256), vm(2, ND, 32, 256), vm(2, ND, 32, 256),
            vm(HALF, 128), vf(D, 8), vf(D, 8), vm(DB, DL),
            vm(2, NB, 96, DL), vm(2, NB, 96, UL), vm(2, NB, 96, LW), vm(NB, 96, DL), vm(NB, 96, UL), vm(NB, 96, LW),
            vm(NY, 96, DL), vm(NY, 96, UL), vm(ND, 48, LW), vm(NY, 96, DL), vm(NY, 96, UL), vm(ND, 48, LW),
            vm(2, 48, DL), vm(2, 96, 384), vm(48, DL), vm(96, 384),
            vm(16, 16, 512), vm(16, 16, 512), vm(16, 16, 128), vm(16, 16, 128),
            dma((SEMS,)), dma((SEMS,)), dma((18,)),
        ],
        compiler_params=pltpu.CompilerParams(
            collective_id=0, has_side_effects=True, vmem_limit_bytes=VMEM_LIMIT
        ),
    )(
        inputs.reshape(ROWS, D), cotangent.reshape(ROWS, D), gain_first, gain_second,
        value_w, gate_w, out_w, up_w, down_w, first_blocks, second_blocks.reshape(512, 64),
        perm_m, expand, perm3, perm12, fold, ufold,
    )
    out, gin, gv, gg, go, gu, gd, g1, g2, gfirst, gsecond = pl.pallas_call(
        finish_kernel,
        out_shape=[
            shape((ROWS, D), BF16), shape((ROWS, D), BF16), shape((3, DB), F32), shape((3, DB), F32), shape((3, DB), F32),
            shape((12, DB), F32), shape((3, HB), F32), shape((1, 3), F32), shape((1, 3), F32), shape((2, 256, 256), F32),
            shape((512, 64), F32),
        ],
        in_specs=any_specs(2) + vmem_specs(4),
        out_specs=any_specs(2) + vmem_specs(9),
        scratch_shapes=[vm(HALF, 128), big(), big(), dma((16,))],
    )(out, gin, mix, early, late, perm_m)
    return (
        out.reshape(1, ROWS, D), gin.reshape(1, ROWS, D), gv.T, gg.T, go.T, gu.T, gd.T, g1.reshape(3), g2.reshape(3),
        gfirst, gsecond.reshape(8, 64, 64),
    )


def solution(mesh):
    tokens, whole = P("dp", "seq", None), P("seq", None, None)
    columns = P(None, ("dp", "seq"))
    gains = P(("dp", "seq"))
    return jax.shard_map(
        body,
        mesh=mesh,
        in_specs=(tokens, tokens, P(), P(), P(), P(), P(), P(), P(), whole, whole),
        out_specs=(tokens, tokens, columns, columns, columns, columns, columns, gains, gains, whole, whole),
        check_vma=False,
    )
```
